32 devices in a mesh: frames: 16 (over z, y, x), strips: 2 (over core).
Axes of the slice: x: 2, y: 2, z: 4, core: 2. Of those that a mesh axis runs over, the one named last changes fastest.
Arguments:
- raw_frames: bfloat16 [1024, 512, 512], P('frames', 'strips'), may hold values from -24 to 24
- dark_frame: float32 [512, 512], P('strips'), may hold values from -6 to 6
- dead_mask: int32 [512, 512], P('strips'), may hold values 0 or 1
- frame_group: int32 [1024], P('frames'), may hold values from 0 to 7
- prior_sigma: float32 [128], replicated, may hold values from 0.2 to 0.5
- start_rotation: float32 [128, 128], replicated, as said below
- basis: bfloat16 [262144, 128], P(('strips', 'frames')), may hold values from -0.01171875 to 0.01171875
Outputs:
- new_basis: bfloat16 [262144, 128], P(('strips', 'frames'))
- new_coeffs: float32 [1024, 128], P('frames')
- new_sigma: float32 [128], replicated
The draws below stay inside these ranges and needn't reach their ends.
Inputs may be any that keep to these rules, and one draw needn't show every extreme that they name: start_rotation is nonsingular.
All inputs are finite; a program needn't handle non-finite values. No bound on the sum of `dead_mask` on one device may be relied on, other than what follows from the above.
Results may differ from the reference program's by a relative error of at most 0.0071.
Values may be sent and summed in bfloat16 or wider, within the bound.
No kernel may reach another device: no remote copies, remote signals or barrier semaphores. Data moves between devices by JAX's collectives and lax.ppermute only.
A program may use at most 192 MiB of HBM per device.

```python
import math
import jax
import jax.numpy as jnp
from jax import lax

H = 512
W = 512
K = 128
F_DEV = 64
GROUPS = 8
ITERS = 4
FRAMES = 1024


def draw_frame_group(key, part):
    frame_index = jnp.arange(FRAMES, dtype=jnp.int32)
    centre = frame_index * GROUPS // FRAMES
    jitter = jax.random.randint(key, (FRAMES,), -2, 3, dtype=jnp.int32)
    group = jnp.clip(centre + jitter, 0, GROUPS - 1)
    group = group.at[0].set(0)
    group = group.at[FRAMES - 1].set(GROUPS - 1)
    return group.astype(jnp.int32)


def draw_start_rotation(key, part):
    position = jnp.arange(K)
    identity = (position[:, None] == position[None, :]).astype(jnp.float32)
    noise = jax.random.normal(key, (K, K), jnp.float32)
    return (identity + 0.25 / math.sqrt(K) * noise).astype(jnp.float32)


def set_ends(entries, rng, least, top_value):
    spot = [jax.random.randint(jax.random.fold_in(rng, axis), (), 0, length) for axis, length in enumerate(entries.shape)]
    longest = entries.shape.index(max(entries.shape))
    beside = spot[:longest] + [(spot[longest] + 1) % entries.shape[longest]] + spot[longest + 1:]
    return entries.at[tuple(spot)].set(least).at[tuple(beside)].set(top_value)


def steps_of(key, shape, cuts, smallest, largest):
    level, own = 1.0, jax.random.fold_in(key, 6)
    for dim, parts in cuts:
        steps = jnp.exp(jax.random.uniform(jax.random.fold_in(own, dim), (parts,), jnp.float32, smallest / len(cuts), largest / len(cuts)))
        level = level * jnp.repeat(steps, shape[dim] // parts).reshape([-1 if axis == dim else 1 for axis in range(len(shape))])
    return level


def normal_values(rng, shape, spread, most, split=(), kind=jnp.bfloat16):
    gain = steps_of(rng, shape, split, -0.22, 0.18) if split else 1.0
    drawn = jax.random.normal(rng, shape, jnp.float32) * spread * gain
    return jnp.minimum(jnp.maximum(drawn, -most), most).astype(kind)


def setup_inputs(seed: int = 0) -> dict:
    keys = jax.random.split(jax.random.key(seed), 8)
    return {
        "raw_frames": normal_values(keys[0], (FRAMES, H, W), 4.0, 24.0, ((0, 16), (1, 2))),
        "dark_frame": normal_values(keys[1], (H, W), 1.0, 6.0, ((0, 2),), jnp.float32),
        "dead_mask": set_ends((jax.random.randint(keys[2], (H, W), 0, 20) < 1).astype(jnp.int32), jax.random.fold_in(keys[2], 1), 0, 1),
        "frame_group": draw_frame_group(jax.random.fold_in(keys[7], 71), 0),
        "prior_sigma": jnp.clip(jnp.exp(jax.random.uniform(keys[4], (K,), jnp.float32, math.log(0.2), math.log(0.5))), 0.2, 0.5),
        "start_rotation": draw_start_rotation(jax.random.fold_in(keys[7], 71), 0),
        "basis": normal_values(keys[6], (H * W, K), (H * W) ** -0.5, 0.01171875, ((0, 32),)),
    }


BLUR_TAPS = (1.0 / 64, 6.0 / 64, 15.0 / 64, 20.0 / 64, 15.0 / 64, 6.0 / 64, 1.0 / 64)
DECAY_RATE = 0.7

def weighted_frames(raw, group, dark_frame, dead_mask):
    corrected = ((raw.astype(jnp.float32) - dark_frame) * (1 - dead_mask).astype(jnp.float32)).astype(jnp.bfloat16)
    corrected = lax.optimization_barrier(corrected).astype(jnp.float32)
    padded = jnp.pad(corrected, ((0, 0), (0, 0), (3, 3)))
    column_blur = BLUR_TAPS[0] * padded[:, :, 0:W]
    for offset in range(1, 7):
        column_blur = column_blur + BLUR_TAPS[offset] * padded[:, :, offset:offset + W]
    padded = jnp.pad(column_blur, ((0, 0), (3, 3), (0, 0)))
    row_blur = BLUR_TAPS[0] * padded[:, 0:H, :]
    for offset in range(1, 7):
        row_blur = row_blur + BLUR_TAPS[offset] * padded[:, offset:offset + H, :]
    frame_weight = jnp.power(jnp.float32(DECAY_RATE), (GROUPS - 1 - group).astype(jnp.float32))
    weighted = (frame_weight[:, None, None] * row_blur).astype(jnp.bfloat16)
    return weighted.reshape(raw.shape[0], H * W)

def orthonormalize(product):
    normal = jnp.dot(product.T, product, precision=lax.Precision.HIGHEST)
    factor = jnp.linalg.cholesky(normal)
    return lax.linalg.triangular_solve(factor, product, left_side=False, lower=True, transpose_a=True)

def reference(raw_frames, dark_frame, dead_mask, frame_group, prior_sigma, start_rotation, basis):
    raw_blocks = raw_frames.reshape(FRAMES // F_DEV, F_DEV, H, W)
    group_blocks = frame_group.reshape(FRAMES // F_DEV, F_DEV)

    def project(item):
        raw, group = item
        weighted = weighted_frames(raw, group, dark_frame, dead_mask)
        return jnp.dot(weighted.astype(jnp.float32), basis.astype(jnp.float32), preferred_element_type=jnp.float32)
    coeffs = lax.map(project, (raw_blocks, group_blocks)).reshape(FRAMES, K)
    gram = jnp.diag(prior_sigma * prior_sigma) + jnp.dot(coeffs.T, coeffs, precision=lax.Precision.HIGHEST) / FRAMES
    rotation = start_rotation
    for step in range(ITERS):
        rotation = orthonormalize(jnp.dot(gram, rotation, precision=lax.Precision.HIGHEST))
    new_coeffs = jnp.dot(coeffs, rotation, precision=lax.Precision.HIGHEST)
    new_basis = jnp.dot(basis.astype(jnp.float32), rotation, precision=lax.Precision.HIGHEST).astype(jnp.bfloat16)
    curved = jnp.dot(gram, rotation, precision=lax.Precision.HIGHEST)
    new_sigma = jnp.sqrt(lax.optimization_barrier(jnp.sum(rotation * curved, axis=0)))
    return (new_basis, new_coeffs, new_sigma)
```

```python
import functools

import jax
import jax.numpy as jnp
from jax import lax
from jax.experimental import pallas as pl
from jax.experimental.pallas import tpu as pltpu
from jax.sharding import PartitionSpec as P

GROUPS = 8
ITERS = 4


BLUR_TAPS = (1.0 / 64, 6.0 / 64, 15.0 / 64, 20.0 / 64, 15.0 / 64, 6.0 / 64, 1.0 / 64)
DECAY_RATE = 0.7
HIGHEST = lax.Precision.HIGHEST
PANEL = 32


def extended(shard, sides, width):
    for axis, dim in sides:
        size, length = (lax.axis_size(axis), shard.shape[dim])
        up = [(i, (i + 1) % size) for i in range(size - 1)]
        down = [(j, i) for i, j in up]
        last = lax.slice_in_dim(shard, length - width, length, axis=dim)
        first = lax.slice_in_dim(shard, 0, width, axis=dim)
        before = lax.ppermute(last, axis, up)
        after = lax.ppermute(first, axis, down)
        shard = jnp.concatenate([before, shard, after], axis=dim)
    return shard


def summed_over(values, axis):
    size = lax.axis_size(axis)
    if size & (size - 1):
        return lax.psum(values, axis)
    distance = 1
    while distance < size:
        pairs = [(i, i ^ distance) for i in range(size)]
        values = values + lax.ppermute(values, axis, pairs)
        distance *= 2
    return values


def reciprocal(values):
    guess = pltpu.reciprocal(values, approx=True)
    return guess * (2.0 - values * guess)


def orthonormal_rows(product):
    size = product.shape[0]
    product = product * lax.rsqrt(jnp.sum(product * product, axis=1, keepdims=True))
    across = (((1,), (1,)), ((), ()))
    down = (((0,), (0,)), ((), ()))
    normal = lax.dot_general(product, product, across, precision=HIGHEST, preferred_element_type=jnp.float32)
    state = jnp.concatenate([normal, product], axis=1)
    rows = lax.broadcasted_iota(jnp.int32, (PANEL, size), 0)
    lanes = lax.broadcasted_iota(jnp.int32, (PANEL, size), 1)
    shape = (PANEL, size)
    finished = []
    for base in range(0, size, PANEL):
        left, right = (state[:PANEL, :size], state[:PANEL, size:])
        for j in range(0, PANEL, 2):
            column = base + j
            col0 = jnp.broadcast_to(left[:, column : column + 1], shape)
            col1 = jnp.broadcast_to(left[:, column + 1 : column + 2], shape)
            aa = jnp.broadcast_to(col0[j : j + 1], shape)
            ab = jnp.broadcast_to(col1[j : j + 1], shape)
            bb = jnp.broadcast_to(col1[j + 1 : j + 2], shape)
            inverse = reciprocal(aa * bb - ab * ab)
            below = rows > j + 1
            second = rows == j + 1
            factor0 = jnp.where(
                below, (col0 * bb - col1 * ab) * inverse, jnp.where(second, ab * reciprocal(aa), 0.0)
            )
            factor1 = jnp.where(below, (col1 * aa - col0 * ab) * inverse, 0.0)
            left0 = jnp.broadcast_to(left[j : j + 1], shape)
            left1 = jnp.broadcast_to(left[j + 1 : j + 2], shape)
            right0 = jnp.broadcast_to(right[j : j + 1], shape)
            right1 = jnp.broadcast_to(right[j + 1 : j + 2], shape)
            left = left - factor0 * left0 - factor1 * left1
            right = right - factor0 * right0 - factor1 * right1
        pivots = jnp.sum(jnp.where(lanes == base + rows, left, 0.0), axis=1, keepdims=True)
        scale = lax.rsqrt(pivots)
        left = left * scale
        right = right * scale
        finished.append(right)
        if base + PANEL < size:
            update = lax.dot_general(
                left[:, base + PANEL :],
                jnp.concatenate([left, right], axis=1),
                down,
                precision=HIGHEST,
                preferred_element_type=jnp.float32,
            )
            state = state[PANEL:] - update
    return jnp.concatenate(finished, axis=0)


def rotate_kernel(frames, chunk, summed_ref, sigma_ref, start_ref, coeffs_ref, basis_ref, basis_out, coeffs_out, sigma_out):
    size = summed_ref.shape[0]
    across = (((1,), (1,)), ((), ()))
    diagonal = lax.broadcasted_iota(jnp.int32, (size, size), 0) == lax.broadcasted_iota(jnp.int32, (size, size), 1)
    sigma = jnp.broadcast_to(sigma_ref[...], (size, size))
    gram = jnp.where(diagonal, sigma * sigma, 0.0) + summed_ref[...] * (1.0 / frames)

    def step(_, turned):
        return orthonormal_rows(jnp.dot(turned, gram, precision=HIGHEST, preferred_element_type=jnp.float32))

    turned = lax.fori_loop(0, ITERS, step, start_ref[...].T)
    coeffs_out[...] = lax.dot_general(
        coeffs_ref[...], turned, across, precision=HIGHEST, preferred_element_type=jnp.float32
    )
    curved = jnp.dot(turned, gram, precision=HIGHEST, preferred_element_type=jnp.float32)
    sigma_out[...] = jnp.sqrt(jnp.sum((turned * curved).T, axis=0, keepdims=True))
    rotation = turned.T
    high = rotation.astype(jnp.bfloat16)
    rest = rotation - high.astype(jnp.float32)
    middle = rest.astype(jnp.bfloat16)
    low = (rest - middle.astype(jnp.float32)).astype(jnp.bfloat16)

    @pl.loop(0, basis_ref.shape[0] // chunk)
    def _(i):
        at = pl.ds(pl.multiple_of(i * chunk, chunk), chunk)
        block = basis_ref[at, :]
        total = jnp.dot(block, low, preferred_element_type=jnp.float32)
        total = total + jnp.dot(block, middle, preferred_element_type=jnp.float32)
        total = total + jnp.dot(block, high, preferred_element_type=jnp.float32)
        basis_out[at, :] = total.astype(basis_out.dtype)


def rotated(summed_gram, total_frames, prior_sigma, start_rotation, coeffs, basis):
    rows, size = basis.shape
    chunk = 512 if rows % 512 == 0 else rows
    new_basis, new_coeffs, new_sigma = pl.pallas_call(
        functools.partial(rotate_kernel, total_frames, chunk),
        out_shape=(
            jax.ShapeDtypeStruct(basis.shape, basis.dtype),
            jax.ShapeDtypeStruct(coeffs.shape, coeffs.dtype),
            jax.ShapeDtypeStruct((1, size), jnp.float32),
        ),
        compiler_params=pltpu.CompilerParams(vmem_limit_bytes=32 * 1024 * 1024),
        name="orthogonal_iteration",
    )(summed_gram, prior_sigma.reshape(1, size), start_rotation, coeffs, basis)
    return (new_basis, new_coeffs, new_sigma.reshape(size))


def body(raw_frames, dark_frame, dead_mask, frame_group, prior_sigma, start_rotation, basis):
    frame_count, strip_rows, columns = raw_frames.shape
    corrected = (
        (raw_frames.astype(jnp.float32) - dark_frame) * (1 - dead_mask).astype(jnp.float32)
    ).astype(jnp.bfloat16)
    position = jnp.arange(columns)
    offsets = position[None, :] - position[:, None]
    banded = jnp.zeros((columns, columns), jnp.float32)
    for shift_by in range(-3, 4):
        banded = banded + jnp.where(offsets == shift_by, BLUR_TAPS[shift_by + 3], 0.0)
    banded = banded.astype(jnp.bfloat16)
    column_blur = jnp.dot(
        corrected.reshape(frame_count * strip_rows, columns),
        banded,
        preferred_element_type=jnp.float32,
    )
    column_blur = column_blur.reshape(frame_count, strip_rows, columns)
    padded = extended(column_blur, (("strips", 1),), 3)
    row_blur = BLUR_TAPS[0] * padded[:, 0:strip_rows, :]
    for offset in range(1, 7):
        row_blur = row_blur + BLUR_TAPS[offset] * padded[:, offset : offset + strip_rows, :]
    frame_weight = jnp.power(
        jnp.float32(DECAY_RATE), (GROUPS - 1 - frame_group).astype(jnp.float32)
    )
    weighted = (
        (frame_weight[:, None, None] * row_blur)
        .astype(jnp.bfloat16)
        .reshape(frame_count, strip_rows * columns)
    )
    partial_value = jnp.dot(
        weighted,
        lax.all_gather(basis, "frames", axis=0, tiled=True),
        preferred_element_type=jnp.float32,
    )
    coeffs = lax.psum(partial_value, "strips")
    total_frames = frame_count * lax.axis_size("frames")
    local_gram = jnp.dot(coeffs.T, coeffs, precision=lax.Precision.HIGHEST)
    summed_gram = summed_over(local_gram, "frames")
    return rotated(summed_gram, total_frames, prior_sigma, start_rotation, coeffs, basis)


def solution(mesh):
    placed = (
        P("frames", "strips", None),
        P("strips", None),
        P("strips", None),
        P("frames"),
        P(),
        P(),
        P(("strips", "frames"), None),
    )
    return jax.shard_map(
        body,
        mesh=mesh,
        in_specs=placed,
        out_specs=(P(("strips", "frames"), None), P("frames", None), P()),
        check_vma=False,
    )
```

```python
import functools

import jax
import jax.numpy as jnp
from jax import lax
from jax.experimental import pallas as pl
from jax.experimental.pallas import tpu as pltpu
from jax.sharding import PartitionSpec as P

GROUPS = 8
ITERS = 4


BLUR_TAPS = (1.0 / 64, 6.0 / 64, 15.0 / 64, 20.0 / 64, 15.0 / 64, 6.0 / 64, 1.0 / 64)
DECAY_RATE = 0.7
HIGHEST = lax.Precision.HIGHEST
PANEL = 32


def extended(shard, sides, width):
    for axis, dim in sides:
        size, length = (lax.axis_size(axis), shard.shape[dim])
        up = [(i, (i + 1) % size) for i in range(size - 1)]
        down = [(j, i) for i, j in up]
        last = lax.slice_in_dim(shard, length - width, length, axis=dim)
        first = lax.slice_in_dim(shard, 0, width, axis=dim)
        before = lax.ppermute(last, axis, up)
        after = lax.ppermute(first, axis, down)
        shard = jnp.concatenate([before, shard, after], axis=dim)
    return shard


def summed_over(values, axis):
    size = lax.axis_size(axis)
    if size & (size - 1):
        return lax.psum(values, axis)
    distance = 1
    while distance < size:
        pairs = [(i, i ^ distance) for i in range(size)]
        values = values + lax.ppermute(values, axis, pairs)
        distance *= 2
    return values


def reciprocal(values):
    guess = pltpu.reciprocal(values, approx=True)
    return guess * (2.0 - values * guess)


def orthonormal_rows(product):
    size = product.shape[0]
    product = product * lax.rsqrt(jnp.sum(product * product, axis=1, keepdims=True))
    across = (((1,), (1,)), ((), ()))
    down = (((0,), (0,)), ((), ()))
    normal = lax.dot_general(product, product, across, precision=HIGHEST, preferred_element_type=jnp.float32)
    state = jnp.concatenate([normal, product], axis=1)
    rows = lax.broadcasted_iota(jnp.int32, (PANEL, size), 0)
    lanes = lax.broadcasted_iota(jnp.int32, (PANEL, size), 1)
    shape = (PANEL, size)
    finished = []
    for base in range(0, size, PANEL):
        left, right = (state[:PANEL, :size], state[:PANEL, size:])
        for j in range(0, PANEL, 2):
            column = base + j
            col0 = jnp.broadcast_to(left[:, column : column + 1], shape)
            col1 = jnp.broadcast_to(left[:, column + 1 : column + 2], shape)
            aa = jnp.broadcast_to(col0[j : j + 1], shape)
            ab = jnp.broadcast_to(col1[j : j + 1], shape)
            bb = jnp.broadcast_to(col1[j + 1 : j + 2], shape)
            inverse = reciprocal(aa * bb - ab * ab)
            below = rows > j + 1
            second = rows == j + 1
            factor0 = jnp.where(
                below, (col0 * bb - col1 * ab) * inverse, jnp.where(second, ab * reciprocal(aa), 0.0)
            )
            factor1 = jnp.where(below, (col1 * aa - col0 * ab) * inverse, 0.0)
            left0 = jnp.broadcast_to(left[j : j + 1], shape)
            left1 = jnp.broadcast_to(left[j + 1 : j + 2], shape)
            right0 = jnp.broadcast_to(right[j : j + 1], shape)
            right1 = jnp.broadcast_to(right[j + 1 : j + 2], shape)
            left = left - factor0 * left0 - factor1 * left1
            right = right - factor0 * right0 - factor1 * right1
        pivots = jnp.sum(jnp.where(lanes == base + rows, left, 0.0), axis=1, keepdims=True)
        scale = lax.rsqrt(pivots)
        left = left * scale
        right = right * scale
        finished.append(right)
        if base + PANEL < size:
            update = lax.dot_general(
                left[:, base + PANEL :],
                jnp.concatenate([left, right], axis=1),
                down,
                precision=HIGHEST,
                preferred_element_type=jnp.float32,
            )
            state = state[PANEL:] - update
    return jnp.concatenate(finished, axis=0)


def rotate_kernel(frames, chunk, summed_ref, sigma_ref, start_ref, coeffs_ref, basis_ref, basis_out, coeffs_out, sigma_out):
    size = summed_ref.shape[0]
    across = (((1,), (1,)), ((), ()))
    diagonal = lax.broadcasted_iota(jnp.int32, (size, size), 0) == lax.broadcasted_iota(jnp.int32, (size, size), 1)
    sigma = jnp.broadcast_to(sigma_ref[...], (size, size))
    gram = jnp.where(diagonal, sigma * sigma, 0.0) + summed_ref[...] * (1.0 / frames)

    def step(_, turned):
        return orthonormal_rows(jnp.dot(turned, gram, precision=HIGHEST, preferred_element_type=jnp.float32))

    turned = lax.fori_loop(0, ITERS, step, start_ref[...].T)
    coeffs_out[...] = lax.dot_general(
        coeffs_ref[...], turned, across, precision=HIGHEST, preferred_element_type=jnp.float32
    )
    curved = jnp.dot(turned, gram, precision=HIGHEST, preferred_element_type=jnp.float32)
    sigma_out[...] = jnp.sqrt(jnp.sum((turned * curved).T, axis=0, keepdims=True))
    rotation = turned.T
    high = rotation.astype(jnp.bfloat16)
    rest = rotation - high.astype(jnp.float32)
    middle = rest.astype(jnp.bfloat16)
    low = (rest - middle.astype(jnp.float32)).astype(jnp.bfloat16)

    @pl.loop(0, basis_ref.shape[0] // chunk)
    def _(i):
        at = pl.ds(pl.multiple_of(i * chunk, chunk), chunk)
        block = basis_ref[at, :]
        total = jnp.dot(block, low, preferred_element_type=jnp.float32)
        total = total + jnp.dot(block, middle, preferred_element_type=jnp.float32)
        total = total + jnp.dot(block, high, preferred_element_type=jnp.float32)
        basis_out[at, :] = total.astype(basis_out.dtype)


def rotated(summed_gram, total_frames, prior_sigma, start_rotation, coeffs, basis):
    rows, size = basis.shape
    chunk = 512 if rows % 512 == 0 else rows
    new_basis, new_coeffs, new_sigma = pl.pallas_call(
        functools.partial(rotate_kernel, total_frames, chunk),
        out_shape=(
            jax.ShapeDtypeStruct(basis.shape, basis.dtype),
            jax.ShapeDtypeStruct(coeffs.shape, coeffs.dtype),
            jax.ShapeDtypeStruct((1, size), jnp.float32),
        ),
        compiler_params=pltpu.CompilerParams(vmem_limit_bytes=32 * 1024 * 1024),
        name="orthogonal_iteration",
    )(summed_gram, prior_sigma.reshape(1, size), start_rotation, coeffs, basis)
    return (new_basis, new_coeffs, new_sigma.reshape(size))


def gathered_body(raw_frames, dark_frame, dead_mask, frame_group, prior_sigma, start_rotation, basis):
    frame_count, strip_rows, columns = raw_frames.shape
    corrected = (
        (raw_frames.astype(jnp.float32) - dark_frame) * (1 - dead_mask).astype(jnp.float32)
    ).astype(jnp.bfloat16)
    position = jnp.arange(columns)
    offsets = position[None, :] - position[:, None]
    banded = jnp.zeros((columns, columns), jnp.float32)
    for shift_by in range(-3, 4):
        banded = banded + jnp.where(offsets == shift_by, BLUR_TAPS[shift_by + 3], 0.0)
    banded = banded.astype(jnp.bfloat16)
    column_blur = jnp.dot(
        corrected.reshape(frame_count * strip_rows, columns),
        banded,
        preferred_element_type=jnp.float32,
    )
    column_blur = column_blur.reshape(frame_count, strip_rows, columns)
    padded = extended(column_blur, (("strips", 1),), 3)
    row_blur = BLUR_TAPS[0] * padded[:, 0:strip_rows, :]
    for offset in range(1, 7):
        row_blur = row_blur + BLUR_TAPS[offset] * padded[:, offset : offset + strip_rows, :]
    frame_weight = jnp.power(
        jnp.float32(DECAY_RATE), (GROUPS - 1 - frame_group).astype(jnp.float32)
    )
    weighted = (
        (frame_weight[:, None, None] * row_blur)
        .astype(jnp.bfloat16)
        .reshape(frame_count, strip_rows * columns)
    )
    partial_value = jnp.dot(
        weighted,
        lax.all_gather(basis, "frames", axis=0, tiled=True),
        preferred_element_type=jnp.float32,
    )
    coeffs = lax.psum(partial_value, "strips")
    total_frames = frame_count * lax.axis_size("frames")
    local_gram = jnp.dot(coeffs.T, coeffs, precision=lax.Precision.HIGHEST)
    summed_gram = summed_over(local_gram, "frames")
    return rotated(summed_gram, total_frames, prior_sigma, start_rotation, coeffs, basis)


RING = (0, 2, 4, 6, 7, 5, 3, 1)
BAND = 16
EDGE = 8
FRAME_BLOCK = 16


def blur_kernel(place_ref, main_ref, prev_ref, next_ref, before_ref, after_ref, dark_ref, keep_ref, banded_ref, weight_ref,
                send_ref, own_ref, rows_ref, lines_ref, blurred_ref):
    pair, side = (place_ref[0], place_ref[1])
    frames, height, columns = main_ref.shape
    span = height + 2 * EDGE
    at = pl.ds(pl.multiple_of(pair * height + BAND - EDGE, EDGE), span)
    dark = dark_ref[at, :]
    keep = keep_ref[at, :]
    top = jnp.where(pair == 0, before_ref[...], prev_ref[...]).astype(jnp.float32)[:, BAND - EDGE :]
    bottom = jnp.where(place_ref[2] == 1, after_ref[...], next_ref[...]).astype(jnp.float32)[:, :EDGE]
    main = (main_ref[...].astype(jnp.float32) - dark[EDGE : EDGE + height]) * keep[EDGE : EDGE + height]
    top = (top - dark[:EDGE]) * keep[:EDGE]
    bottom = (bottom - dark[EDGE + height :]) * keep[EDGE + height :]
    tiles = columns // 128
    flat_ref = rows_ref.reshape(tiles * frames * span, 128)
    for tile in range(tiles):
        part = slice(tile * 128, (tile + 1) * 128)
        rows_ref[tile, :, :EDGE] = top[:, :, part]
        rows_ref[tile, :, EDGE : EDGE + height] = main[:, :, part]
        rows_ref[tile, :, EDGE + height :] = bottom[:, :, part]
        for row in range(height + 6):
            line = flat_ref[pl.ds(tile * frames * span + row + EDGE - 3, frames, stride=span), :]
            lines_ref[row * frames : (row + 1) * frames, part] = line.astype(jnp.bfloat16)
    blurred_ref[...] = jnp.dot(lines_ref[...], banded_ref[...], preferred_element_type=jnp.float32)
    weight = jnp.broadcast_to(weight_ref[:, :1], (frames, columns))
    for out_ref, first in ((send_ref, (1 - side) * BAND), (own_ref, side * BAND)):
        for row in range(BAND):
            parts = [
                blurred_ref[pl.ds(pl.multiple_of((first + row + offset) * frames, frames), frames), :]
                for offset in range(7)
            ]
            total = BLUR_TAPS[3] * parts[3]
            for offset in range(3):
                total = total + BLUR_TAPS[offset] * (parts[offset] + parts[6 - offset])
            out_ref[row] = (weight * total).astype(jnp.bfloat16)


def blurred_bands(place, raw_frames, before, after, dark, keep, banded, weight):
    frame_count, strip_rows, columns = raw_frames.shape
    bands = strip_rows // BAND
    height = 2 * BAND
    fixed = lambda f, place: (0, 0)
    grid_spec = pltpu.PrefetchScalarGridSpec(
        num_scalar_prefetch=1,
        grid=(frame_count // FRAME_BLOCK,),
        in_specs=[
            pl.BlockSpec((FRAME_BLOCK, height, columns), lambda f, place: (f, place[0], 0)),
            pl.BlockSpec((FRAME_BLOCK, BAND, columns), lambda f, place: (f, jnp.maximum(2 * place[0] - 1, 0), 0)),
            pl.BlockSpec((FRAME_BLOCK, BAND, columns), lambda f, place: (f, jnp.minimum(2 * place[0] + 2, bands - 1), 0)),
            pl.BlockSpec((FRAME_BLOCK, BAND, columns), lambda f, place: (f, 0, 0)),
            pl.BlockSpec((FRAME_BLOCK, BAND, columns), lambda f, place: (f, 0, 0)),
            pl.BlockSpec(dark.shape, fixed),
            pl.BlockSpec(keep.shape, fixed),
            pl.BlockSpec(banded.shape, fixed),
            pl.BlockSpec((FRAME_BLOCK, weight.shape[1]), lambda f, place: (f, 0)),
        ],
        out_specs=[pl.BlockSpec((BAND, FRAME_BLOCK, columns), lambda f, place: (0, f, 0))] * 2,
        scratch_shapes=[
            pltpu.VMEM((columns // 128, FRAME_BLOCK, height + 2 * EDGE, 128), jnp.float32),
            pltpu.VMEM(((height + 6) * FRAME_BLOCK, columns), jnp.bfloat16),
            pltpu.VMEM(((height + 6) * FRAME_BLOCK, columns), jnp.float32),
        ],
    )
    shape = jax.ShapeDtypeStruct((BAND, frame_count, columns), jnp.bfloat16)
    return pl.pallas_call(
        blur_kernel,
        grid_spec=grid_spec,
        out_shape=(shape, shape),
        compiler_params=pltpu.CompilerParams(vmem_limit_bytes=32 * 1024 * 1024),
        cost_estimate=pl.CostEstimate(
            flops=2 * frame_count * height * columns * columns, bytes_accessed=8 * frame_count * height * columns,
            transcendentals=0,
        ),
        name="blur_bands",
    )(place, raw_frames, raw_frames, raw_frames, before, after, dark, keep, banded, weight)


def project_kernel(total_ref, own_ref, came_ref, basis_ref, out_ref):
    columns = own_ref.shape[2]

    @pl.when(pl.program_id(0) == 0)
    def _():
        out_ref[...] = total_ref[...]

    total = out_ref[...]
    for row in range(own_ref.shape[0]):
        lines = jnp.concatenate([own_ref[row], came_ref[row]], axis=0)
        total = total + jnp.dot(
            lines, basis_ref[row * columns : (row + 1) * columns, :], preferred_element_type=jnp.float32
        )
    out_ref[...] = total


def projected(total, own, came, basis, first_row):
    step = 4
    _, frame_count, columns = own.shape
    size = basis.shape[1]
    skipped = first_row // step
    steps = basis.shape[0] // columns // step
    lines = pl.BlockSpec((step, frame_count, columns), lambda i: (i + skipped, 0, 0))
    whole = pl.BlockSpec(total.shape, lambda i: (0, 0))
    return pl.pallas_call(
        project_kernel,
        grid=(steps,),
        in_specs=[whole, lines, lines, pl.BlockSpec((step * columns, size), lambda i: (i, 0))],
        out_specs=whole,
        out_shape=jax.ShapeDtypeStruct(total.shape, jnp.float32),
        compiler_params=pltpu.CompilerParams(vmem_limit_bytes=32 * 1024 * 1024),
        cost_estimate=pl.CostEstimate(
            flops=4 * frame_count * basis.shape[0] * size, bytes_accessed=4 * own.size + 2 * basis.size, transcendentals=0
        ),
        name="project_band",
    )(total, own, came, basis)


def paired_body(raw_frames, dark_frame, dead_mask, frame_group, prior_sigma, start_rotation, basis):
    frame_count, strip_rows, columns = raw_frames.shape
    size = basis.shape[1]
    count = lax.axis_size("frames")
    strips = lax.axis_size("strips")
    ring = len(RING)
    index = lax.axis_index("frames")
    side = index % 2
    position = jnp.array([RING.index(pair) for pair in range(ring)], jnp.int32)[index // 2]
    pair_at = jnp.array(RING, jnp.int32)

    def links(by):
        return [
            (2 * RING[at] + x, 2 * RING[(at + by) % ring] + x) for at in range(ring) for x in range(2)
        ]

    swap = [(i, i ^ 1) for i in range(count)]
    ahead = [(i, i + 1) for i in range(strips - 1)]
    back = [(i + 1, i) for i in range(strips - 1)]
    move = lambda values, pairs: lax.ppermute(values, "frames", pairs)
    before = lax.ppermute(raw_frames[:, strip_rows - BAND :], "strips", ahead)
    after = lax.ppermute(raw_frames[:, :BAND], "strips", back)
    keep_frame = (1 - dead_mask).astype(jnp.float32)
    both = jnp.concatenate([dark_frame, keep_frame], axis=1)
    edge_before = lax.ppermute(both[strip_rows - BAND :], "strips", ahead)
    edge_after = lax.ppermute(both[:BAND], "strips", back)
    both = jnp.concatenate([edge_before, both, edge_after], axis=0)
    dark, keep = (both[:, :columns], both[:, columns:])
    column = jnp.arange(columns)
    offsets = column[None, :] - column[:, None]
    banded = jnp.zeros((columns, columns), jnp.float32)
    for shift_by in range(-3, 4):
        banded = banded + jnp.where(offsets == shift_by, BLUR_TAPS[shift_by + 3], 0.0)
    banded = banded.astype(jnp.bfloat16)
    frame_weight = jnp.power(jnp.float32(DECAY_RATE), (GROUPS - 1 - frame_group).astype(jnp.float32))
    weight = jnp.broadcast_to(frame_weight[:, None], (frame_count, 128))

    def bands(offset):
        pair = pair_at[(position + offset) % ring]
        place = jnp.stack([pair, side, (pair == ring - 1).astype(jnp.int32)]).astype(jnp.int32)
        return blurred_bands(place, raw_frames, before, after, dark, keep, banded, weight)

    order = (0, -1, 1, -2, 2, -3, 3, 4)
    half = basis.shape[0] // 2
    blocks = {0: (basis,)}
    own, send, came = ([], [], [])
    total = jnp.zeros((2 * frame_count, size), jnp.float32)
    up, down = (basis, basis)
    used = 0

    def project(total, slot):
        row = 0
        for block in blocks[order[slot]]:
            total = projected(total, own[slot], came[slot], block, row)
            row += block.shape[0] // columns
        return total

    for stage in range(4):
        if stage < 3:
            up, down = (move(up, links(1)), move(down, links(-1)))
        else:
            up, down = (move(up[:half], links(1)), move(down[half:], links(-1)))
        for slot in (2 * stage, 2 * stage + 1):
            if slot >= len(own):
                sent, kept = bands(order[slot])
                own.append(kept)
                send.append(sent)
            came.append(move(send[slot], swap))
        while stage < 2 and len(own) < (4, 8)[stage]:
            sent, kept = bands(order[len(own)])
            own.append(kept)
            send.append(sent)
        if stage > 0:
            for slot in (2 * stage - 2, 2 * stage - 1):
                total = project(total, slot)
        last = 2 * stage
        held = (up, down, total, came[last], came[last + 1]) + tuple(send[last + 2 :]) + tuple(own[last + 2 :])
        up, down, total, came[last], came[last + 1], *others = lax.optimization_barrier(held)
        waiting = len(send) - last - 2
        send[last + 2 :] = others[:waiting]
        own[last + 2 :] = others[waiting:]
        if stage < 3:
            blocks[-stage - 1], blocks[stage + 1] = ((up,), (down,))
        else:
            blocks[4] = (up, down)
    for slot in (6, 7):
        total = project(total, slot)
    total = total + lax.ppermute(total, "strips", [(i, i ^ 1) for i in range(strips)])
    other = move(total, swap)
    mine = total[:frame_count] + other[frame_count:]
    theirs = total[frame_count:] + other[:frame_count]
    gram = jnp.dot(mine.T, mine, precision=HIGHEST) + jnp.dot(theirs.T, theirs, precision=HIGHEST)
    distance = 2
    while distance < count:
        gram = gram + move(gram, [(i, i ^ distance) for i in range(count)])
        distance *= 2
    return rotated(gram, frame_count * count, prior_sigma, start_rotation, mine, basis)


def body(raw_frames, *others):
    _, strip_rows, columns = raw_frames.shape
    paired = lax.axis_size("frames") == 2 * len(RING) and lax.axis_size("strips") == 2
    if paired and strip_rows == 2 * len(RING) * BAND and raw_frames.shape[0] % FRAME_BLOCK == 0:
        return paired_body(raw_frames, *others)
    return gathered_body(raw_frames, *others)


def solution(mesh):
    placed = (
        P("frames", "strips", None),
        P("strips", None),
        P("strips", None),
        P("frames"),
        P(),
        P(),
        P(("strips", "frames"), None),
    )
    return jax.shard_map(
        body,
        mesh=mesh,
        in_specs=placed,
        out_specs=(P(("strips", "frames"), None), P("frames", None), P()),
        check_vma=False,
    )
```

```python
import functools

import jax
import jax.numpy as jnp
import numpy as np
from jax import lax
from jax.experimental import pallas as pl
from jax.experimental.pallas import tpu as pltpu
from jax.sharding import PartitionSpec as P

GROUPS = 8
ITERS = 4


BLUR_TAPS = (1.0 / 64, 6.0 / 64, 15.0 / 64, 20.0 / 64, 15.0 / 64, 6.0 / 64, 1.0 / 64)
DECAY_RATE = 0.7
HIGHEST = lax.Precision.HIGHEST
PANEL = 64
VMEM_BYTES = 32 * 1024 * 1024
BLUR_BYTES = 49 * 1024 * 1024


def extended(shard, sides, width):
    for axis, dim in sides:
        size, length = (lax.axis_size(axis), shard.shape[dim])
        up = [(i, (i + 1) % size) for i in range(size - 1)]
        down = [(j, i) for i, j in up]
        last = lax.slice_in_dim(shard, length - width, length, axis=dim)
        first = lax.slice_in_dim(shard, 0, width, axis=dim)
        before = lax.ppermute(last, axis, up)
        after = lax.ppermute(first, axis, down)
        shard = jnp.concatenate([before, shard, after], axis=dim)
    return shard


def summed_over(values, axis):
    size = lax.axis_size(axis)
    if size & (size - 1):
        return lax.psum(values, axis)
    distance = 1
    while distance < size:
        pairs = [(i, i ^ distance) for i in range(size)]
        values = values + lax.ppermute(values, axis, pairs)
        distance *= 2
    return values


def reciprocal(values):
    guess = pltpu.reciprocal(values, approx=True)
    return guess * (2.0 - values * guess)


def orthonormal_rows(product):
    size = product.shape[0]
    product = product * lax.rsqrt(jnp.sum(product * product, axis=1, keepdims=True))
    across = (((1,), (1,)), ((), ()))
    down = (((0,), (0,)), ((), ()))
    normal = lax.dot_general(product, product, across, precision=HIGHEST, preferred_element_type=jnp.float32)
    state = jnp.concatenate([normal, product], axis=1)
    shape = (PANEL, size)
    rows = lax.broadcasted_iota(jnp.int32, shape, 0)
    lanes = lax.broadcasted_iota(jnp.int32, shape, 1)
    finished = []
    for base in range(0, size, PANEL):
        left, right = (state[:PANEL, :size], state[:PANEL, size:])
        for j in range(0, PANEL, 4):
            at = base + j
            col = [jnp.broadcast_to(left[:, at + i : at + i + 1], shape) for i in range(4)]
            p = {(r, s): jnp.broadcast_to(col[s][j + r : j + r + 1], shape) for s in range(4) for r in range(s + 1)}
            inverse = reciprocal(p[0, 0] * p[1, 1] - p[0, 1] * p[0, 1])
            a00, a01, a11 = (p[1, 1] * inverse, -p[0, 1] * inverse, p[0, 0] * inverse)
            t00, t10 = (a00 * p[0, 2] + a01 * p[1, 2], a01 * p[0, 2] + a11 * p[1, 2])
            t01, t11 = (a00 * p[0, 3] + a01 * p[1, 3], a01 * p[0, 3] + a11 * p[1, 3])
            q00 = p[2, 2] - p[0, 2] * t00 - p[1, 2] * t10
            q01 = p[2, 3] - p[0, 2] * t01 - p[1, 2] * t11
            q11 = p[3, 3] - p[0, 3] * t01 - p[1, 3] * t11
            inverse = reciprocal(q00 * q11 - q01 * q01)
            b00, b01, b11 = (q11 * inverse, -q01 * inverse, q00 * inverse)
            first = p[0, 1] * reciprocal(p[0, 0])
            third = q01 * reciprocal(q00)
            col2 = col[2] - col[0] * t00 - col[1] * t10
            col3 = col[3] - col[0] * t01 - col[1] * t11
            f2 = col2 * b00 + col3 * b01
            f3 = col2 * b01 + col3 * b11
            f0 = col[0] * a00 + col[1] * a01 - f2 * t00 - f3 * t01
            f1 = col[0] * a01 + col[1] * a11 - f2 * t10 - f3 * t11
            below = rows > j + 3
            row1, row2, row3 = (rows == j + 1, rows == j + 2, rows == j + 3)
            zero = jnp.zeros(shape, jnp.float32)
            inner = jnp.where(row2, t00, jnp.where(row3, t01 - third * t00, zero))
            f0 = jnp.where(below, f0, jnp.where(row1, first, inner))
            f1 = jnp.where(below, f1, jnp.where(row2, t10, jnp.where(row3, t11 - third * t10, zero)))
            f2 = jnp.where(below, f2, jnp.where(row3, third, zero))
            f3 = jnp.where(below, f3, zero)
            lines = [jnp.broadcast_to(left[j + i : j + i + 1], shape) for i in range(4)]
            left = left - ((f0 * lines[0] + f1 * lines[1]) + (f2 * lines[2] + f3 * lines[3]))
            lines = [jnp.broadcast_to(right[j + i : j + i + 1], shape) for i in range(4)]
            right = right - ((f0 * lines[0] + f1 * lines[1]) + (f2 * lines[2] + f3 * lines[3]))
        pivots = jnp.sum(jnp.where(lanes == base + rows, left, 0.0), axis=1, keepdims=True)
        scale = lax.rsqrt(pivots)
        left = left * scale
        right = right * scale
        finished.append(right)
        if base + PANEL < size:
            update = lax.dot_general(
                left[:, base + PANEL :],
                jnp.concatenate([left, right], axis=1),
                down,
                precision=HIGHEST,
                preferred_element_type=jnp.float32,
            )
            state = state[PANEL:] - update
    return jnp.concatenate(finished, axis=0)


def rotate_kernel(frames, chunk, summed_ref, more_ref, sigma_ref, start_ref, coeffs_ref, basis_ref, basis_out, coeffs_out, sigma_out,
                  held_ref, turned_ref, come_sem, go_sem):
    come = pltpu.make_async_copy(basis_ref, held_ref, come_sem)
    come.start()
    size = summed_ref.shape[0]
    across = (((1,), (1,)), ((), ()))
    diagonal = lax.broadcasted_iota(jnp.int32, (size, size), 0) == lax.broadcasted_iota(jnp.int32, (size, size), 1)
    sigma = jnp.broadcast_to(sigma_ref[...], (size, size))
    gram = jnp.where(diagonal, sigma * sigma, 0.0) + (summed_ref[...] + more_ref[...]) * (1.0 / frames)

    def step(_, turned):
        return orthonormal_rows(jnp.dot(turned, gram, precision=HIGHEST, preferred_element_type=jnp.float32))

    turned = lax.fori_loop(0, ITERS, step, start_ref[...].T)
    rotation = turned.T
    high = rotation.astype(jnp.bfloat16)
    low = (rotation - high.astype(jnp.float32)).astype(jnp.bfloat16)
    pair = jnp.concatenate([high, low], axis=1)
    come.wait()
    goes = []
    for i in range(held_ref.shape[0] // chunk):
        at = pl.ds(i * chunk, chunk)
        total = jnp.dot(held_ref[at, :], pair, preferred_element_type=jnp.float32)
        turned_ref[at, :] = (total[:, :size] + total[:, size:]).astype(turned_ref.dtype)
        goes.append(pltpu.make_async_copy(turned_ref.at[at, :], basis_out.at[at, :], go_sem.at[i]))
        goes[-1].start()
    coeffs_out[...] = lax.dot_general(
        coeffs_ref[...], turned, across, precision=HIGHEST, preferred_element_type=jnp.float32
    )
    curved = jnp.dot(turned, gram, precision=HIGHEST, preferred_element_type=jnp.float32)
    sigma_out[...] = jnp.sqrt(jnp.sum((turned * curved).T, axis=0, keepdims=True))
    for go in goes:
        go.wait()


def rotated(summed_gram, more_gram, total_frames, prior_sigma, start_rotation, coeffs, basis):
    rows, size = basis.shape
    chunk = 1024 if rows % 1024 == 0 else rows
    inside = pl.BlockSpec(memory_space=pltpu.VMEM)
    outside = pl.BlockSpec(memory_space=pl.ANY)
    new_basis, new_coeffs, new_sigma = pl.pallas_call(
        functools.partial(rotate_kernel, total_frames, chunk),
        in_specs=[inside, inside, inside, inside, inside, outside],
        out_specs=(outside, inside, inside),
        out_shape=(
            jax.ShapeDtypeStruct(basis.shape, basis.dtype),
            jax.ShapeDtypeStruct(coeffs.shape, coeffs.dtype),
            jax.ShapeDtypeStruct((1, size), jnp.float32),
        ),
        scratch_shapes=[
            pltpu.VMEM(basis.shape, basis.dtype),
            pltpu.VMEM(basis.shape, basis.dtype),
            pltpu.SemaphoreType.DMA,
            pltpu.SemaphoreType.DMA((rows // chunk,)),
        ],
        compiler_params=pltpu.CompilerParams(vmem_limit_bytes=VMEM_BYTES),
        name="orthogonal_iteration",
    )(summed_gram, more_gram, prior_sigma.reshape(1, size), start_rotation, coeffs, basis)
    return (new_basis, new_coeffs, new_sigma.reshape(size))


def gathered_body(raw_frames, dark_frame, dead_mask, frame_group, prior_sigma, start_rotation, basis):
    frame_count, strip_rows, columns = raw_frames.shape
    corrected = (
        (raw_frames.astype(jnp.float32) - dark_frame) * (1 - dead_mask).astype(jnp.float32)
    ).astype(jnp.bfloat16)
    position = jnp.arange(columns)
    offsets = position[None, :] - position[:, None]
    banded = jnp.zeros((columns, columns), jnp.float32)
    for shift_by in range(-3, 4):
        banded = banded + jnp.where(offsets == shift_by, BLUR_TAPS[shift_by + 3], 0.0)
    banded = banded.astype(jnp.bfloat16)
    column_blur = jnp.dot(
        corrected.reshape(frame_count * strip_rows, columns),
        banded,
        preferred_element_type=jnp.float32,
    )
    column_blur = column_blur.reshape(frame_count, strip_rows, columns)
    padded = extended(column_blur, (("strips", 1),), 3)
    row_blur = BLUR_TAPS[0] * padded[:, 0:strip_rows, :]
    for offset in range(1, 7):
        row_blur = row_blur + BLUR_TAPS[offset] * padded[:, offset : offset + strip_rows, :]
    frame_weight = jnp.power(
        jnp.float32(DECAY_RATE), (GROUPS - 1 - frame_group).astype(jnp.float32)
    )
    weighted = (
        (frame_weight[:, None, None] * row_blur)
        .astype(jnp.bfloat16)
        .reshape(frame_count, strip_rows * columns)
    )
    partial_value = jnp.dot(
        weighted,
        lax.all_gather(basis, "frames", axis=0, tiled=True),
        preferred_element_type=jnp.float32,
    )
    coeffs = lax.psum(partial_value, "strips")
    total_frames = frame_count * lax.axis_size("frames")
    local_gram = jnp.dot(coeffs.T, coeffs, precision=lax.Precision.HIGHEST)
    summed_gram = summed_over(local_gram, "frames")
    return rotated(summed_gram, jnp.zeros_like(summed_gram), total_frames, prior_sigma, start_rotation, coeffs, basis)


RING = (0, 2, 4, 6, 7, 5, 3, 1)
PLACES = 4 * len(RING) + 2
BAND = 16
EDGE = 8
FRAME_BLOCK = 16


def entry(place, at):
    return place[1 + place[0] * PLACES + at]


def blur_kernel(slot, outputs, begin, place_ref, group_ref, main_ref, prev_ref, next_ref, *refs):
    edge_ref, refs = (refs[0], refs[1:]) if slot else (None, refs)
    darks, masks, banded_ref, refs = (refs[:3], refs[3:6], refs[6], refs[7:])
    out_refs, (rows_ref, lines_ref, blurred_ref) = (refs[: len(outputs)], refs[len(outputs) :])
    side = entry(place_ref, 4 * slot + 2)
    frames, height, columns = main_ref.shape
    span = height + 2 * EDGE
    parts = [main_ref[...], prev_ref[...], next_ref[...]]
    main, top, bottom = [
        (part.astype(jnp.float32) - dark_ref[...]) * (1 - mask_ref[...]).astype(jnp.float32)
        for part, dark_ref, mask_ref in zip(parts, darks, masks)
    ]
    top, bottom = (top[:, BAND - EDGE :], bottom[:, :EDGE])
    if slot:
        upper = entry(place_ref, 0) == 0
        edge = edge_ref[...].astype(jnp.float32)
        top = jnp.where(entry(place_ref, 4 * slot + 3) == 1, jnp.where(upper, 0.0, edge[:, BAND - EDGE :]), top)
        bottom = jnp.where(entry(place_ref, 4 * slot + 4) == 1, jnp.where(upper, edge[:, :EDGE], 0.0), bottom)
    tiles = columns // 128
    flat_ref = rows_ref.reshape(tiles * frames * span, 128)
    for tile in range(tiles):
        part = slice(tile * 128, (tile + 1) * 128)
        rows_ref[tile, :, :EDGE] = top[:, :, part]
        rows_ref[tile, :, EDGE : EDGE + height] = main[:, :, part]
        rows_ref[tile, :, EDGE + height :] = bottom[:, :, part]
        for row in range(height + 6):
            line = flat_ref[pl.ds(tile * frames * span + row + EDGE - 3, frames, stride=span), :]
            lines_ref[row * frames : (row + 1) * frames, part] = line.astype(jnp.bfloat16)
    blurred_ref[...] = jnp.dot(lines_ref[...], banded_ref[...], preferred_element_type=jnp.float32)
    frame = lax.broadcasted_iota(jnp.int32, (frames, columns), 0)
    group = jnp.zeros((frames, columns), jnp.int32)
    for i in range(frames):
        group = jnp.where(frame == i, group_ref[pl.program_id(0) * frames + (begin + i)], group)
    weight = jnp.ones((frames, columns), jnp.float32)
    for value in range(GROUPS - 1):
        weight = jnp.where(group == value, DECAY_RATE ** (GROUPS - 1 - value), weight)
    for name, out_ref in zip(outputs, out_refs):
        first = 0 if len(outputs) == 1 else (side if name == "own" else 1 - side) * BAND
        for row in range(BAND):
            taken = [
                blurred_ref[pl.ds(pl.multiple_of((first + row + offset) * frames, frames), frames), :]
                for offset in range(7)
            ]
            total = BLUR_TAPS[3] * taken[3]
            for offset in range(3):
                total = total + BLUR_TAPS[offset] * (taken[offset] + taken[6 - offset])
            out_ref[row] = (weight * total).astype(jnp.bfloat16)


def blurred_bands(slot, outputs, begin, frame_count, place, raw_frames, edge, dark_frame, dead_mask, banded, frame_group):
    _, strip_rows, columns = raw_frames.shape
    bands = strip_rows // BAND
    height = len(outputs) * BAND
    skipped = begin // FRAME_BLOCK
    lines = height + 6

    def at_main(place):
        if len(outputs) == 2:
            return entry(place, 4 * slot + 1)
        side = entry(place, 4 * slot + 2)
        return 2 * entry(place, 4 * slot + 1) + (side if outputs[0] == "own" else 1 - side)

    at_prev = lambda place: jnp.maximum(len(outputs) * at_main(place) - 1, 0)
    at_next = lambda place: jnp.minimum(len(outputs) * (at_main(place) + 1), bands - 1)
    rows = ((height, at_main), (BAND, at_prev), (BAND, at_next))
    edges = () if edge is None else (edge,)

    def pixels(size, at):
        return pl.BlockSpec((size, columns), lambda f, place, group: (at(place), 0))

    def frames(size, at):
        return pl.BlockSpec((FRAME_BLOCK, size, columns), lambda f, place, group: (f + skipped, at(place), 0))

    grid_spec = pltpu.PrefetchScalarGridSpec(
        num_scalar_prefetch=2,
        grid=(frame_count // FRAME_BLOCK,),
        in_specs=[frames(*row) for row in rows]
        + [frames(BAND, lambda place: 0)] * len(edges)
        + [pixels(*row) for row in rows] * 2
        + [pl.BlockSpec(banded.shape, lambda f, place, group: (0, 0))],
        out_specs=[pl.BlockSpec((BAND, FRAME_BLOCK, columns), lambda f, place, group: (0, f, 0))] * len(outputs),
        scratch_shapes=[
            pltpu.VMEM((columns // 128, FRAME_BLOCK, height + 2 * EDGE, 128), jnp.float32),
            pltpu.VMEM((lines * FRAME_BLOCK, columns), jnp.bfloat16),
            pltpu.VMEM((lines * FRAME_BLOCK, columns), jnp.float32),
        ],
    )
    shape = jax.ShapeDtypeStruct((BAND, frame_count, columns), jnp.bfloat16)
    starts = slot == 0 and outputs[0] == "sent"
    return pl.pallas_call(
        functools.partial(blur_kernel, slot, outputs, begin),
        grid_spec=grid_spec,
        out_shape=[shape] * len(outputs),
        compiler_params=pltpu.CompilerParams(vmem_limit_bytes=60 * 1024 * 1024 if starts else BLUR_BYTES),
        cost_estimate=pl.CostEstimate(flops=1024, bytes_accessed=1024, transcendentals=0),
        name="blur_bands",
    )(place, frame_group, *[raw_frames] * 3, *edges, *[dark_frame] * 3, *[dead_mask] * 3, banded)


def project_kernel(slot, at, parts, place_ref, total_ref, *refs):
    line_refs, basis_refs, out_ref = (refs[:parts], refs[parts:-1], refs[-1])
    columns = line_refs[0].shape[2]

    @pl.when(pl.program_id(0) == 0)
    def _():
        out_ref[...] = total_ref[...]

    def add(basis_ref):
        total = out_ref[at, :]
        for row in range(line_refs[0].shape[0]):
            lines = jnp.concatenate([line_ref[row] for line_ref in line_refs], axis=0)
            total = total + jnp.dot(
                lines, basis_ref[row * columns : (row + 1) * columns, :], preferred_element_type=jnp.float32
            )
        out_ref[at, :] = total

    if len(basis_refs) == 1:
        add(basis_refs[0])
    else:
        here = entry(place_ref, PLACES - 1) == slot
        pl.when(here)(lambda: add(basis_refs[0]))
        pl.when(jnp.logical_not(here))(lambda: add(basis_refs[1]))


def projected(total, own, came, basis, first_row, choice=None):
    step = 4
    begin = 0 if own else total.shape[0] // 2
    lines = (*own, *came)
    columns = lines[0].shape[2]
    at = slice(begin, begin + sum(values.shape[1] for values in lines))
    size = basis.shape[1]
    skipped = first_row // step
    steps = basis.shape[0] // columns // step
    whole = pl.BlockSpec(total.shape, lambda i, place: (0, 0))
    other, place, slot = choice or (None, jnp.zeros((1,), jnp.int32), 0)
    blocks = (basis,) if choice is None else (basis, other)
    return pl.pallas_call(
        functools.partial(project_kernel, slot, at, len(lines)),
        grid_spec=pltpu.PrefetchScalarGridSpec(
            num_scalar_prefetch=1,
            grid=(steps,),
            in_specs=[whole]
            + [pl.BlockSpec((step, *values.shape[1:]), lambda i, place: (i + skipped, 0, 0)) for values in lines]
            + [pl.BlockSpec((step * columns, size), lambda i, place: (i, 0))] * len(blocks),
            out_specs=whole,
        ),
        out_shape=jax.ShapeDtypeStruct(total.shape, jnp.float32),
        compiler_params=pltpu.CompilerParams(vmem_limit_bytes=VMEM_BYTES),
        cost_estimate=pl.CostEstimate(flops=1024, bytes_accessed=1024, transcendentals=0),
        name="project_band",
    )(place, total, *lines, *blocks)


def merge_kernel(total_ref, strip_ref, side_ref, both_ref, coeffs_out, gram_out):
    half = coeffs_out.shape[0]
    down = (((0,), (0,)), ((), ()))
    near = total_ref[...] + strip_ref[...]
    far = side_ref[...] + both_ref[...]
    grams = []
    for at, other in ((slice(0, half), slice(half, None)), (slice(half, None), slice(0, half))):
        coeffs = near[at] + far[other]
        if not grams:
            coeffs_out[...] = coeffs
        grams.append(lax.dot_general(coeffs, coeffs, down, precision=HIGHEST, preferred_element_type=jnp.float32))
    gram_out[...] = grams[0] + grams[1]


def placement():
    ring = len(RING)
    table = np.zeros((2 * ring, 2, PLACES), np.int32)
    for at in range(ring):
        order = [0, -1, 1, -2, 2, -3, 3, 4]
        if RING[at] in (0, ring - 1):
            order[:2] = order[1::-1]
        for strip in range(2):
            for x in range(2):
                row = table[2 * RING[at] + x, strip]
                row[0], row[-1] = (strip, order.index(0))
                for slot, by in enumerate(order):
                    pair = RING[(at + by) % ring]
                    row[4 * slot + 1 : 4 * slot + 5] = (pair, x, pair == 0, pair == ring - 1)
    return table.reshape(-1)


def paired_body(raw_frames, dark_frame, dead_mask, frame_group, prior_sigma, start_rotation, basis):
    frame_count, strip_rows, columns = raw_frames.shape
    size = basis.shape[1]
    count = lax.axis_size("frames")
    strips = lax.axis_size("strips")
    ring = len(RING)
    strip = lax.axis_index("strips")
    index = lax.axis_index(("frames", "strips"))
    place = jnp.concatenate([index.reshape(1).astype(jnp.int32), jnp.asarray(placement())])

    def links(by):
        return [
            (2 * RING[at] + x, 2 * RING[(at + by) % ring] + x) for at in range(ring) for x in range(2)
        ]

    swap = [(i, i ^ 1) for i in range(count)]
    move = lambda values, pairs: lax.ppermute(values, "frames", pairs)
    column = np.arange(columns)
    taps = np.array(BLUR_TAPS + (0.0,), np.float32)
    offsets = column[None, :] - column[:, None] + 3
    banded = jnp.asarray(taps[np.where((offsets >= 0) & (offsets < 7), offsets, 7)], jnp.bfloat16)

    def bands(slot, outputs, edge, begin=0, held=frame_count):
        return blurred_bands(
            slot, outputs, begin, held, place, raw_frames, edge, dark_frame, dead_mask, banded, frame_group
        )

    first = frame_count // 2
    (sent_first,) = bands(0, ("sent",), None, 0, first)
    sent_first, near_raw, near_dark, near_mask = lax.optimization_barrier(
        (sent_first, raw_frames, dark_frame, dead_mask)
    )
    came_first = move(sent_first, swap)
    (sent_rest,) = bands(0, ("sent",), None, first, first)
    near = jnp.where(strip == 0, strip_rows - BAND, 0)
    rows = [lax.dynamic_slice_in_dim(values, near, BAND, axis=-2) for values in (near_raw, near_dark, near_mask)]
    border = ((rows[0].astype(jnp.float32) - rows[1]) * (1 - rows[2]).astype(jnp.float32)).astype(jnp.bfloat16)
    came_first, sent_rest, border = lax.optimization_barrier((came_first, sent_rest, border))
    came_rest = move(sent_rest, swap)
    edge = lax.ppermute(border, "strips", [(0, 1), (1, 0)])
    sent_next, own_next = bands(1, ("sent", "own"), edge)
    came_rest, sent_next, own_next, passing = lax.optimization_barrier((came_rest, sent_next, own_next, basis))
    half = basis.shape[0] // 2
    blocks = {0: basis}
    send, own, came = ([None, sent_next], [None, own_next], [came_rest])
    total = jnp.zeros((2 * frame_count, size), jnp.float32)
    up, down = (passing, passing)

    def project(total, slot):
        parts = (came[slot],) if slot else (came_first, came[0])
        if slot < 2:
            return projected(total, (own[slot],), parts, blocks[0], 0, (blocks[-1], place, slot))
        return projected(total, (own[slot],), parts, blocks[(0, -1, 1, -2, 2, -3, 3)[slot]], 0)

    for stage in range(4):
        if stage < 3:
            up, down = (move(up, links(1)), move(down, links(-1)))
        else:
            up, down = (move(up[:half], links(1)), move(down[half:], links(-1)))
        for slot in range(len(came), min(2 * stage + 3, ring)):
            if slot == len(send):
                sent, kept = bands(slot, ("sent", "own"), edge)
                own.append(kept)
                send.append(sent)
            came.append(move(send[slot], swap))
        if stage == 0:
            (own[0],) = bands(0, ("own",), None)
        while stage < 2 and len(own) < (5, 8)[stage]:
            sent, kept = bands(len(own), ("sent", "own"), edge)
            own.append(kept)
            send.append(sent)
        for slot in ((), (0, 1, 2), (3, 4), (5, 6))[stage]:
            total = project(total, slot)
        if stage == 3:
            break
        last = len(came)
        held = (up, down, total, came[last - 2], came[last - 1]) + tuple(send[last:]) + tuple(own[last:])
        up, down, total, came[last - 2], came[last - 1], *others = lax.optimization_barrier(held)
        waiting = len(send) - last
        send[last:] = others[:waiting]
        own[last:] = others[waiting:]
        blocks[-stage - 1], blocks[stage + 1] = (up, down)
    for lines in (((own[7],), ()), ((), (came[7],))):
        for n, block in enumerate((up, down)):
            total = projected(total, *lines, block, n * BAND // 2)
    flips = [
        lax.ppermute(total, ("frames", "strips"), [(i, i ^ flip) for i in range(count * strips)]) for flip in (1, 2, 3)
    ]
    coeffs, gram = pl.pallas_call(
        merge_kernel,
        out_shape=(
            jax.ShapeDtypeStruct((frame_count, size), jnp.float32),
            jax.ShapeDtypeStruct((size, size), jnp.float32),
        ),
        name="merge",
    )(total, *flips)
    near = [move(gram, [(i, i ^ flip) for i in range(count)]) for flip in (2, 4, 6)]
    gram = (gram + near[0]) + (near[1] + near[2])
    far = move(gram, [(i, i ^ 8) for i in range(count)])
    return rotated(gram, far, frame_count * count, prior_sigma, start_rotation, coeffs, basis)


def body(raw_frames, *others):
    _, strip_rows, columns = raw_frames.shape
    paired = lax.axis_size("frames") == 2 * len(RING) and lax.axis_size("strips") == 2
    if paired and strip_rows == 2 * len(RING) * BAND and raw_frames.shape[0] % FRAME_BLOCK == 0:
        return paired_body(raw_frames, *others)
    return gathered_body(raw_frames, *others)


def solution(mesh):
    placed = (
        P("frames", "strips", None),
        P("strips", None),
        P("strips", None),
        P("frames"),
        P(),
        P(),
        P(("strips", "frames"), None),
    )
    return jax.shard_map(
        body,
        mesh=mesh,
        in_specs=placed,
        out_specs=(P(("strips", "frames"), None), P("frames", None), P()),
        check_vma=False,
    )
```

```python
import functools

import jax
import jax.numpy as jnp
import numpy as np
from jax import lax
from jax.experimental import pallas as pl
from jax.experimental.pallas import tpu as pltpu
from jax.sharding import PartitionSpec as P

GROUPS = 8
ITERS = 4


BLUR_TAPS = (1.0 / 64, 6.0 / 64, 15.0 / 64, 20.0 / 64, 15.0 / 64, 6.0 / 64, 1.0 / 64)
DECAY_RATE = 0.7
HIGHEST = lax.Precision.HIGHEST
PANEL = 64
BLOCK = 8
VMEM_BYTES = 32 * 1024 * 1024
BLUR_BYTES = 49 * 1024 * 1024


def extended(shard, sides, width):
    for axis, dim in sides:
        size, length = (lax.axis_size(axis), shard.shape[dim])
        up = [(i, (i + 1) % size) for i in range(size - 1)]
        down = [(j, i) for i, j in up]
        last = lax.slice_in_dim(shard, length - width, length, axis=dim)
        first = lax.slice_in_dim(shard, 0, width, axis=dim)
        before = lax.ppermute(last, axis, up)
        after = lax.ppermute(first, axis, down)
        shard = jnp.concatenate([before, shard, after], axis=dim)
    return shard


def summed_over(values, axis):
    size = lax.axis_size(axis)
    if size & (size - 1):
        return lax.psum(values, axis)
    distance = 1
    while distance < size:
        pairs = [(i, i ^ distance) for i in range(size)]
        values = values + lax.ppermute(values, axis, pairs)
        distance *= 2
    return values


def reciprocal(values):
    guess = pltpu.reciprocal(values, approx=True)
    return guess * (2.0 - values * guess)


def orthonormal_rows(product):
    size = product.shape[0]
    product = product * lax.rsqrt(jnp.sum(product * product, axis=1, keepdims=True))
    across = (((1,), (1,)), ((), ()))
    down = (((0,), (0,)), ((), ()))
    normal = lax.dot_general(product, product, across, precision=HIGHEST, preferred_element_type=jnp.float32)
    state = jnp.concatenate([normal, product], axis=1)
    shape = (BLOCK, size)
    rows = lax.broadcasted_iota(jnp.int32, shape, 0)
    lanes = lax.broadcasted_iota(jnp.int32, shape, 1)
    wide = lambda values: jnp.broadcast_to(values, shape)
    finished = []
    for base in range(0, size, PANEL):
        left = [state[row : row + BLOCK, :size] for row in range(0, PANEL, BLOCK)]
        right = [state[row : row + BLOCK, size:] for row in range(0, PANEL, BLOCK)]
        for at in range(PANEL // BLOCK):
            column = base + at * BLOCK
            below = range(at + 1, PANEL // BLOCK)
            col = [
                {i: wide(left[i][:, column + s : column + s + 1]) for i in (at, *below)} for s in range(BLOCK)
            ]
            p = {(r, s): wide(col[s][at][r : r + 1]) for s in range(BLOCK) for r in range(s + 1)}
            lines = [(wide(left[at][s : s + 1]), wide(right[at][s : s + 1])) for s in range(BLOCK)]
            for u in range(0, BLOCK, 2):
                v = u + 1
                inverse = reciprocal(p[u, u] * p[v, v] - p[u, v] * p[u, v])
                a00, a01, a11 = (p[v, v] * inverse, -p[u, v] * inverse, p[u, u] * inverse)
                within = p[u, v] * reciprocal(p[u, u])
                later = range(v + 1, BLOCK)
                t0 = {s: a00 * p[u, s] + a01 * p[v, s] for s in later}
                t1 = {s: a01 * p[u, s] + a11 * p[v, s] for s in later}
                for s in later:
                    for r in range(v + 1, s + 1):
                        p[r, s] = p[r, s] - (p[u, r] * t0[s] + p[v, r] * t1[s])
                    for i in below:
                        col[s][i] = col[s][i] - (col[u][i] * t0[s] + col[v][i] * t1[s])
                    lines[s] = tuple(
                        line - (t0[s] * first + t1[s] * second)
                        for line, first, second in zip(lines[s], lines[u], lines[v])
                    )
                for i in below:
                    f0 = col[u][i] * a00 + col[v][i] * a01
                    f1 = col[u][i] * a01 + col[v][i] * a11
                    left[i] = left[i] - (f0 * lines[u][0] + f1 * lines[v][0])
                    right[i] = right[i] - (f0 * lines[u][1] + f1 * lines[v][1])
                lines[v] = tuple(second - within * first for first, second in zip(lines[u], lines[v]))
            new_left, new_right = lines[0]
            for s in range(1, BLOCK):
                new_left = jnp.where(rows == s, lines[s][0], new_left)
                new_right = jnp.where(rows == s, lines[s][1], new_right)
            pivots = jnp.sum(jnp.where(lanes == column + rows, new_left, 0.0), axis=1, keepdims=True)
            scale = lax.rsqrt(pivots)
            left[at] = new_left * scale
            right[at] = new_right * scale
        left = jnp.concatenate(left, axis=0)
        right = jnp.concatenate(right, axis=0)
        finished.append(right)
        if base + PANEL < size:
            update = lax.dot_general(
                left[:, base + PANEL :],
                jnp.concatenate([left, right], axis=1),
                down,
                precision=HIGHEST,
                preferred_element_type=jnp.float32,
            )
            state = state[PANEL:] - update
    return jnp.concatenate(finished, axis=0)


def packed(matrix):
    half = matrix.shape[0] // 2
    rows = lax.broadcasted_iota(jnp.int32, (half, 2 * half), 0)
    lanes = lax.broadcasted_iota(jnp.int32, (half, 2 * half), 1)
    lower = pltpu.roll(matrix[half:], half, 1)
    diagonal = jnp.sum(jnp.where(lanes == rows, lower, 0.0), axis=0, keepdims=True)
    return jnp.concatenate(
        [jnp.where(lanes < rows, lower, matrix[:half]), jnp.broadcast_to(diagonal, (BLOCK, 2 * half))], axis=0
    )


def unpacked(values):
    size = values.shape[1]
    half = size // 2
    rows = lax.broadcasted_iota(jnp.int32, (half, size), 0)
    lanes = lax.broadcasted_iota(jnp.int32, (half, size), 1)
    entries = values[:half]
    diagonal = jnp.broadcast_to(values[half : half + 1], (half, size))
    lower = jnp.where(lanes < rows, entries, jnp.where(lanes == rows, diagonal, 0.0))
    part = jnp.concatenate([jnp.where(lanes >= rows, entries, 0.0), pltpu.roll(lower, half, 1)], axis=0)
    on = lax.broadcasted_iota(jnp.int32, (size, size), 0) == lax.broadcasted_iota(jnp.int32, (size, size), 1)
    return part + part.T - jnp.where(on, part, 0.0)


def rotate_kernel(frames, chunk, summed_ref, more_ref, sigma_ref, start_ref, coeffs_ref, basis_ref, basis_out, coeffs_out, sigma_out,
                  held_ref, turned_ref, come_sem, go_sem):
    come = pltpu.make_async_copy(basis_ref, held_ref, come_sem)
    come.start()
    size = summed_ref.shape[1]
    across = (((1,), (1,)), ((), ()))
    diagonal = lax.broadcasted_iota(jnp.int32, (size, size), 0) == lax.broadcasted_iota(jnp.int32, (size, size), 1)
    sigma = jnp.broadcast_to(sigma_ref[...], (size, size))
    gram = jnp.where(diagonal, sigma * sigma, 0.0) + unpacked(summed_ref[...] + more_ref[...]) * (1.0 / frames)

    def step(_, turned):
        return orthonormal_rows(jnp.dot(turned, gram, precision=HIGHEST, preferred_element_type=jnp.float32))

    turned = lax.fori_loop(0, ITERS, step, start_ref[...].T)
    rotation = turned.T
    high = rotation.astype(jnp.bfloat16)
    low = (rotation - high.astype(jnp.float32)).astype(jnp.bfloat16)
    pair = jnp.concatenate([high, low], axis=1)
    come.wait()
    goes = []
    for i in range(held_ref.shape[0] // chunk):
        at = pl.ds(i * chunk, chunk)
        total = jnp.dot(held_ref[at, :], pair, preferred_element_type=jnp.float32)
        turned_ref[at, :] = (total[:, :size] + total[:, size:]).astype(turned_ref.dtype)
        goes.append(pltpu.make_async_copy(turned_ref.at[at, :], basis_out.at[at, :], go_sem.at[i]))
        goes[-1].start()
    coeffs_out[...] = lax.dot_general(
        coeffs_ref[...], turned, across, precision=HIGHEST, preferred_element_type=jnp.float32
    )
    curved = jnp.dot(turned, gram, precision=HIGHEST, preferred_element_type=jnp.float32)
    sigma_out[...] = jnp.sqrt(jnp.sum((turned * curved).T, axis=0, keepdims=True))
    for go in goes:
        go.wait()


def rotated(summed_gram, more_gram, total_frames, prior_sigma, start_rotation, coeffs, basis):
    rows, size = basis.shape
    chunk = 1024 if rows % 1024 == 0 else rows
    inside = pl.BlockSpec(memory_space=pltpu.VMEM)
    outside = pl.BlockSpec(memory_space=pl.ANY)
    new_basis, new_coeffs, new_sigma = pl.pallas_call(
        functools.partial(rotate_kernel, total_frames, chunk),
        in_specs=[inside, inside, inside, inside, inside, outside],
        out_specs=(outside, inside, inside),
        out_shape=(
            jax.ShapeDtypeStruct(basis.shape, basis.dtype),
            jax.ShapeDtypeStruct(coeffs.shape, coeffs.dtype),
            jax.ShapeDtypeStruct((1, size), jnp.float32),
        ),
        scratch_shapes=[
            pltpu.VMEM(basis.shape, basis.dtype),
            pltpu.VMEM(basis.shape, basis.dtype),
            pltpu.SemaphoreType.DMA,
            pltpu.SemaphoreType.DMA((rows // chunk,)),
        ],
        compiler_params=pltpu.CompilerParams(vmem_limit_bytes=VMEM_BYTES),
        name="orthogonal_iteration",
    )(summed_gram, more_gram, prior_sigma.reshape(1, size), start_rotation, coeffs, basis)
    return (new_basis, new_coeffs, new_sigma.reshape(size))


def packed_alone(matrix):
    def kernel(matrix_ref, out_ref):
        out_ref[...] = packed(matrix_ref[...])

    size = matrix.shape[0]
    shape = jax.ShapeDtypeStruct((size // 2 + BLOCK, size), jnp.float32)
    return pl.pallas_call(kernel, out_shape=shape, name="pack")(matrix)


def gathered_body(raw_frames, dark_frame, dead_mask, frame_group, prior_sigma, start_rotation, basis):
    frame_count, strip_rows, columns = raw_frames.shape
    corrected = (
        (raw_frames.astype(jnp.float32) - dark_frame) * (1 - dead_mask).astype(jnp.float32)
    ).astype(jnp.bfloat16)
    position = jnp.arange(columns)
    offsets = position[None, :] - position[:, None]
    banded = jnp.zeros((columns, columns), jnp.float32)
    for shift_by in range(-3, 4):
        banded = banded + jnp.where(offsets == shift_by, BLUR_TAPS[shift_by + 3], 0.0)
    banded = banded.astype(jnp.bfloat16)
    column_blur = jnp.dot(
        corrected.reshape(frame_count * strip_rows, columns),
        banded,
        preferred_element_type=jnp.float32,
    )
    column_blur = column_blur.reshape(frame_count, strip_rows, columns)
    padded = extended(column_blur, (("strips", 1),), 3)
    row_blur = BLUR_TAPS[0] * padded[:, 0:strip_rows, :]
    for offset in range(1, 7):
        row_blur = row_blur + BLUR_TAPS[offset] * padded[:, offset : offset + strip_rows, :]
    frame_weight = jnp.power(
        jnp.float32(DECAY_RATE), (GROUPS - 1 - frame_group).astype(jnp.float32)
    )
    weighted = (
        (frame_weight[:, None, None] * row_blur)
        .astype(jnp.bfloat16)
        .reshape(frame_count, strip_rows * columns)
    )
    partial_value = jnp.dot(
        weighted,
        lax.all_gather(basis, "frames", axis=0, tiled=True),
        preferred_element_type=jnp.float32,
    )
    coeffs = lax.psum(partial_value, "strips")
    total_frames = frame_count * lax.axis_size("frames")
    local_gram = jnp.dot(coeffs.T, coeffs, precision=lax.Precision.HIGHEST)
    summed_gram = summed_over(local_gram, "frames")
    summed_gram = packed_alone(summed_gram)
    return rotated(summed_gram, jnp.zeros_like(summed_gram), total_frames, prior_sigma, start_rotation, coeffs, basis)


RING = (0, 2, 4, 6, 7, 5, 3, 1)
PLACES = 4 * len(RING) + 2
BAND = 16
EDGE = 8
FRAME_BLOCK = 16


def entry(place, at):
    index, table = place
    return table[index[0] * PLACES + at]


def blur_kernel(slot, outputs, begin, index_ref, table_ref, group_ref, main_ref, prev_ref, next_ref, *refs):
    place = (index_ref, table_ref)
    edge_ref, refs = (refs[0], refs[1:]) if slot else (None, refs)
    darks, masks, banded_ref, refs = (refs[:3], refs[3:6], refs[6], refs[7:])
    out_refs, (rows_ref, lines_ref, blurred_ref) = (refs[: len(outputs)], refs[len(outputs) :])
    side = entry(place, 4 * slot + 2)
    frames, height, columns = main_ref.shape
    span = height + 2 * EDGE
    parts = [main_ref[...], prev_ref[...], next_ref[...]]
    main, top, bottom = [
        (part.astype(jnp.float32) - dark_ref[...]) * (1 - mask_ref[...]).astype(jnp.float32)
        for part, dark_ref, mask_ref in zip(parts, darks, masks)
    ]
    top, bottom = (top[:, BAND - EDGE :], bottom[:, :EDGE])
    if slot:
        upper = entry(place, 0) == 0
        edge = edge_ref[...].astype(jnp.float32)
        top = jnp.where(entry(place, 4 * slot + 3) == 1, jnp.where(upper, 0.0, edge[:, BAND - EDGE :]), top)
        bottom = jnp.where(entry(place, 4 * slot + 4) == 1, jnp.where(upper, edge[:, :EDGE], 0.0), bottom)
    tiles = columns // 128
    flat_ref = rows_ref.reshape(tiles * frames * span, 128)
    for tile in range(tiles):
        part = slice(tile * 128, (tile + 1) * 128)
        rows_ref[tile, :, :EDGE] = top[:, :, part]
        rows_ref[tile, :, EDGE : EDGE + height] = main[:, :, part]
        rows_ref[tile, :, EDGE + height :] = bottom[:, :, part]
        for row in range(height + 6):
            line = flat_ref[pl.ds(tile * frames * span + row + EDGE - 3, frames, stride=span), :]
            lines_ref[row * frames : (row + 1) * frames, part] = line.astype(jnp.bfloat16)
    blurred_ref[...] = jnp.dot(lines_ref[...], banded_ref[...], preferred_element_type=jnp.float32)
    frame = lax.broadcasted_iota(jnp.int32, (frames, columns), 0)
    group = jnp.zeros((frames, columns), jnp.int32)
    for i in range(frames):
        group = jnp.where(frame == i, group_ref[pl.program_id(0) * frames + (begin + i)], group)
    weight = jnp.ones((frames, columns), jnp.float32)
    for value in range(GROUPS - 1):
        weight = jnp.where(group == value, DECAY_RATE ** (GROUPS - 1 - value), weight)
    for name, out_ref in zip(outputs, out_refs):
        first = 0 if len(outputs) == 1 else (side if name == "own" else 1 - side) * BAND
        for row in range(BAND):
            taken = [
                blurred_ref[pl.ds(pl.multiple_of((first + row + offset) * frames, frames), frames), :]
                for offset in range(7)
            ]
            total = BLUR_TAPS[3] * taken[3]
            for offset in range(3):
                total = total + BLUR_TAPS[offset] * (taken[offset] + taken[6 - offset])
            out_ref[row] = (weight * total).astype(jnp.bfloat16)


def blurred_bands(slot, outputs, begin, frame_count, place, raw_frames, edge, dark_frame, dead_mask, banded, frame_group):
    _, strip_rows, columns = raw_frames.shape
    bands = strip_rows // BAND
    height = len(outputs) * BAND
    skipped = begin // FRAME_BLOCK
    lines = height + 6

    def at_main(place):
        if len(outputs) == 2:
            return entry(place, 4 * slot + 1)
        side = entry(place, 4 * slot + 2)
        return 2 * entry(place, 4 * slot + 1) + (side if outputs[0] == "own" else 1 - side)

    at_prev = lambda place: jnp.maximum(len(outputs) * at_main(place) - 1, 0)
    at_next = lambda place: jnp.minimum(len(outputs) * (at_main(place) + 1), bands - 1)
    rows = ((height, at_main), (BAND, at_prev), (BAND, at_next))
    edges = () if edge is None else (edge,)

    def pixels(size, at):
        return pl.BlockSpec((size, columns), lambda f, index, table, group: (at((index, table)), 0))

    def frames(size, at):
        return pl.BlockSpec((FRAME_BLOCK, size, columns), lambda f, index, table, group: (f + skipped, at((index, table)), 0))

    grid_spec = pltpu.PrefetchScalarGridSpec(
        num_scalar_prefetch=3,
        grid=(frame_count // FRAME_BLOCK,),
        in_specs=[frames(*row) for row in rows]
        + [frames(BAND, lambda place: 0)] * len(edges)
        + [pixels(*row) for row in rows] * 2
        + [pl.BlockSpec(banded.shape, lambda f, index, table, group: (0, 0))],
        out_specs=[pl.BlockSpec((BAND, FRAME_BLOCK, columns), lambda f, index, table, group: (0, f, 0))] * len(outputs),
        scratch_shapes=[
            pltpu.VMEM((columns // 128, FRAME_BLOCK, height + 2 * EDGE, 128), jnp.float32),
            pltpu.VMEM((lines * FRAME_BLOCK, columns), jnp.bfloat16),
            pltpu.VMEM((lines * FRAME_BLOCK, columns), jnp.float32),
        ],
    )
    shape = jax.ShapeDtypeStruct((BAND, frame_count, columns), jnp.bfloat16)
    starts = slot == 0 and outputs[0] == "sent"
    return pl.pallas_call(
        functools.partial(blur_kernel, slot, outputs, begin),
        grid_spec=grid_spec,
        out_shape=[shape] * len(outputs),
        compiler_params=pltpu.CompilerParams(vmem_limit_bytes=60 * 1024 * 1024 if starts else BLUR_BYTES),
        cost_estimate=pl.CostEstimate(flops=1024, bytes_accessed=1024, transcendentals=0),
        name="blur_bands",
    )(*place, frame_group, *[raw_frames] * 3, *edges, *[dark_frame] * 3, *[dead_mask] * 3, banded)


def project_kernel(slot, at, parts, index_ref, table_ref, total_ref, *refs):
    line_refs, basis_refs, out_ref = (refs[:parts], refs[parts:-1], refs[-1])
    columns = line_refs[0].shape[2]

    @pl.when(pl.program_id(0) == 0)
    def _():
        out_ref[...] = total_ref[...]

    def add(basis_ref):
        total = out_ref[at, :]
        for row in range(line_refs[0].shape[0]):
            lines = jnp.concatenate([line_ref[row] for line_ref in line_refs], axis=0)
            total = total + jnp.dot(
                lines, basis_ref[row * columns : (row + 1) * columns, :], preferred_element_type=jnp.float32
            )
        out_ref[at, :] = total

    if len(basis_refs) == 1:
        add(basis_refs[0])
    else:
        here = entry((index_ref, table_ref), PLACES - 1) == slot
        pl.when(here)(lambda: add(basis_refs[0]))
        pl.when(jnp.logical_not(here))(lambda: add(basis_refs[1]))


def projected(total, own, came, basis, first_row, choice=None):
    step = 4
    begin = 0 if own else total.shape[0] // 2
    lines = (*own, *came)
    columns = lines[0].shape[2]
    at = slice(begin, begin + sum(values.shape[1] for values in lines))
    size = basis.shape[1]
    skipped = first_row // step
    steps = basis.shape[0] // columns // step
    whole = pl.BlockSpec(total.shape, lambda i, index, table: (0, 0))
    other, place, slot = choice or (None, [jnp.zeros((1,), jnp.int32)] * 2, 0)
    blocks = (basis,) if choice is None else (basis, other)
    return pl.pallas_call(
        functools.partial(project_kernel, slot, at, len(lines)),
        grid_spec=pltpu.PrefetchScalarGridSpec(
            num_scalar_prefetch=2,
            grid=(steps,),
            in_specs=[whole]
            + [pl.BlockSpec((step, *values.shape[1:]), lambda i, index, table: (i + skipped, 0, 0)) for values in lines]
            + [pl.BlockSpec((step * columns, size), lambda i, index, table: (i, 0))] * len(blocks),
            out_specs=whole,
        ),
        out_shape=jax.ShapeDtypeStruct(total.shape, jnp.float32),
        compiler_params=pltpu.CompilerParams(vmem_limit_bytes=VMEM_BYTES),
        cost_estimate=pl.CostEstimate(flops=1024, bytes_accessed=1024, transcendentals=0),
        name="project_band",
    )(*place, total, *lines, *blocks)


def merge_kernel(total_ref, strip_ref, side_ref, both_ref, coeffs_out, gram_out):
    half = coeffs_out.shape[0]
    down = (((0,), (0,)), ((), ()))
    near = total_ref[...] + strip_ref[...]
    far = side_ref[...] + both_ref[...]
    grams = []
    for at, other in ((slice(0, half), slice(half, None)), (slice(half, None), slice(0, half))):
        coeffs = near[at] + far[other]
        if not grams:
            coeffs_out[...] = coeffs
        grams.append(lax.dot_general(coeffs, coeffs, down, precision=HIGHEST, preferred_element_type=jnp.float32))
    gram_out[...] = packed(grams[0] + grams[1])


def placement():
    ring = len(RING)
    table = np.zeros((2 * ring, 2, PLACES), np.int32)
    for at in range(ring):
        order = [0, -1, 1, -2, 2, -3, 3, 4]
        if RING[at] in (0, ring - 1):
            order[:2] = order[1::-1]
        for strip in range(2):
            for x in range(2):
                row = table[2 * RING[at] + x, strip]
                row[0], row[-1] = (strip, order.index(0))
                for slot, by in enumerate(order):
                    pair = RING[(at + by) % ring]
                    row[4 * slot + 1 : 4 * slot + 5] = (pair, x, pair == 0, pair == ring - 1)
    return table.reshape(-1)


def paired_body(raw_frames, dark_frame, dead_mask, frame_group, prior_sigma, start_rotation, basis):
    frame_count, strip_rows, columns = raw_frames.shape
    size = basis.shape[1]
    count = lax.axis_size("frames")
    strips = lax.axis_size("strips")
    ring = len(RING)
    strip = lax.axis_index("strips")
    index = lax.axis_index(("frames", "strips"))
    place = (index.reshape(1).astype(jnp.int32), jnp.asarray(placement()))

    def links(by):
        return [
            (2 * RING[at] + x, 2 * RING[(at + by) % ring] + x) for at in range(ring) for x in range(2)
        ]

    swap = [(i, i ^ 1) for i in range(count)]
    move = lambda values, pairs: lax.ppermute(values, "frames", pairs)
    column = np.arange(columns)
    taps = np.array(BLUR_TAPS + (0.0,), np.float32)
    offsets = column[None, :] - column[:, None] + 3
    banded = jnp.asarray(taps[np.where((offsets >= 0) & (offsets < 7), offsets, 7)], jnp.bfloat16)

    def bands(slot, outputs, edge, begin=0, held=frame_count):
        return blurred_bands(
            slot, outputs, begin, held, place, raw_frames, edge, dark_frame, dead_mask, banded, frame_group
        )

    first = frame_count // 2
    (sent_first,) = bands(0, ("sent",), None, 0, first)
    sent_first, near_raw, near_dark, near_mask = lax.optimization_barrier(
        (sent_first, raw_frames, dark_frame, dead_mask)
    )
    came_first = move(sent_first, swap)
    (sent_rest,) = bands(0, ("sent",), None, first, first)
    near = jnp.where(strip == 0, strip_rows - BAND, 0)
    rows = [lax.dynamic_slice_in_dim(values, near, BAND, axis=-2) for values in (near_raw, near_dark, near_mask)]
    border = ((rows[0].astype(jnp.float32) - rows[1]) * (1 - rows[2]).astype(jnp.float32)).astype(jnp.bfloat16)
    came_first, sent_rest, border = lax.optimization_barrier((came_first, sent_rest, border))
    came_rest = move(sent_rest, swap)
    edge = lax.ppermute(border, "strips", [(0, 1), (1, 0)])
    sent_next, own_next = bands(1, ("sent", "own"), edge)
    came_rest, sent_next, own_next, passing = lax.optimization_barrier((came_rest, sent_next, own_next, basis))
    half = basis.shape[0] // 2
    blocks = {0: basis}
    send, own, came = ([None, sent_next], [None, own_next], [came_rest])
    total = jnp.zeros((2 * frame_count, size), jnp.float32)
    up, down = (passing, passing)

    def project(total, slot):
        parts = (came[slot],) if slot else (came_first, came[0])
        if slot < 2:
            return projected(total, (own[slot],), parts, blocks[0], 0, (blocks[-1], place, slot))
        return projected(total, (own[slot],), parts, blocks[(0, -1, 1, -2, 2, -3, 3)[slot]], 0)

    for stage in range(4):
        if stage < 3:
            up, down = (move(up, links(1)), move(down, links(-1)))
        else:
            up, down = (move(up[:half], links(1)), move(down[half:], links(-1)))
        for slot in range(len(came), min(2 * stage + 3, ring)):
            if slot == len(send):
                sent, kept = bands(slot, ("sent", "own"), edge)
                own.append(kept)
                send.append(sent)
            came.append(move(send[slot], swap))
        if stage == 0:
            (own[0],) = bands(0, ("own",), None)
        while stage < 2 and len(own) < (5, 8)[stage]:
            sent, kept = bands(len(own), ("sent", "own"), edge)
            own.append(kept)
            send.append(sent)
        for slot in ((), (0, 1, 2), (3, 4), (5, 6))[stage]:
            total = project(total, slot)
        if stage == 3:
            break
        last = len(came)
        held = (up, down, total, came[last - 2], came[last - 1]) + tuple(send[last:]) + tuple(own[last:])
        up, down, total, came[last - 2], came[last - 1], *others = lax.optimization_barrier(held)
        waiting = len(send) - last
        send[last:] = others[:waiting]
        own[last:] = others[waiting:]
        blocks[-stage - 1], blocks[stage + 1] = (up, down)
    for lines in (((own[7],), ()), ((), (came[7],))):
        for n, block in enumerate((up, down)):
            total = projected(total, *lines, block, n * BAND // 2)
    flips = [
        lax.ppermute(total, ("frames", "strips"), [(i, i ^ flip) for i in range(count * strips)]) for flip in (1, 2, 3)
    ]
    coeffs, gram = pl.pallas_call(
        merge_kernel,
        out_shape=(
            jax.ShapeDtypeStruct((frame_count, size), jnp.float32),
            jax.ShapeDtypeStruct((size // 2 + BLOCK, size), jnp.float32),
        ),
        name="merge",
    )(total, *flips)
    near = [move(gram, [(i, i ^ flip) for i in range(count)]) for flip in (2, 4, 6)]
    gram = (gram + near[0]) + (near[1] + near[2])
    far = move(gram, [(i, i ^ 8) for i in range(count)])
    return rotated(gram, far, frame_count * count, prior_sigma, start_rotation, coeffs, basis)


def body(raw_frames, *others):
    _, strip_rows, columns = raw_frames.shape
    paired = lax.axis_size("frames") == 2 * len(RING) and lax.axis_size("strips") == 2
    if paired and strip_rows == 2 * len(RING) * BAND and raw_frames.shape[0] % FRAME_BLOCK == 0:
        return paired_body(raw_frames, *others)
    return gathered_body(raw_frames, *others)


def solution(mesh):
    placed = (
        P("frames", "strips", None),
        P("strips", None),
        P("strips", None),
        P("frames"),
        P(),
        P(),
        P(("strips", "frames"), None),
    )
    return jax.shard_map(
        body,
        mesh=mesh,
        in_specs=placed,
        out_specs=(P(("strips", "frames"), None), P("frames", None), P()),
        check_vma=False,
    )
```

```python
import functools

import jax
import jax.numpy as jnp
import numpy as np
from jax import lax
from jax.experimental import pallas as pl
from jax.experimental.pallas import tpu as pltpu
from jax.sharding import PartitionSpec as P

GROUPS = 8
ITERS = 4


BLUR_TAPS = (1.0 / 64, 6.0 / 64, 15.0 / 64, 20.0 / 64, 15.0 / 64, 6.0 / 64, 1.0 / 64)
DECAY_RATE = 0.7
HIGHEST = lax.Precision.HIGHEST
PANEL = 64
BLOCK = 8
VMEM_BYTES = 32 * 1024 * 1024
BLUR_BYTES = 49 * 1024 * 1024


def extended(shard, sides, width):
    for axis, dim in sides:
        size, length = (lax.axis_size(axis), shard.shape[dim])
        up = [(i, (i + 1) % size) for i in range(size - 1)]
        down = [(j, i) for i, j in up]
        last = lax.slice_in_dim(shard, length - width, length, axis=dim)
        first = lax.slice_in_dim(shard, 0, width, axis=dim)
        before = lax.ppermute(last, axis, up)
        after = lax.ppermute(first, axis, down)
        shard = jnp.concatenate([before, shard, after], axis=dim)
    return shard


def summed_over(values, axis):
    size = lax.axis_size(axis)
    if size & (size - 1):
        return lax.psum(values, axis)
    distance = 1
    while distance < size:
        pairs = [(i, i ^ distance) for i in range(size)]
        values = values + lax.ppermute(values, axis, pairs)
        distance *= 2
    return values


def reciprocal(values):
    guess = pltpu.reciprocal(values, approx=True)
    return guess * (2.0 - values * guess)


def orthonormal_rows(product):
    size = product.shape[0]
    product = product * lax.rsqrt(jnp.sum(product * product, axis=1, keepdims=True))
    across = (((1,), (1,)), ((), ()))
    down = (((0,), (0,)), ((), ()))
    normal = lax.dot_general(product, product, across, precision=HIGHEST, preferred_element_type=jnp.float32)
    state = jnp.concatenate([normal, product], axis=1)
    shape = (BLOCK, size)
    rows = lax.broadcasted_iota(jnp.int32, shape, 0)
    lanes = lax.broadcasted_iota(jnp.int32, shape, 1)
    wide = lambda values: jnp.broadcast_to(values, shape)
    finished = []
    for base in range(0, size, PANEL):
        left = [state[row : row + BLOCK, :size] for row in range(0, PANEL, BLOCK)]
        right = [state[row : row + BLOCK, size:] for row in range(0, PANEL, BLOCK)]
        for at in range(PANEL // BLOCK):
            column = base + at * BLOCK
            below = range(at + 1, PANEL // BLOCK)
            col = [
                {i: wide(left[i][:, column + s : column + s + 1]) for i in (at, *below)} for s in range(BLOCK)
            ]
            p = {(r, s): wide(col[s][at][r : r + 1]) for s in range(BLOCK) for r in range(s + 1)}
            lines = [(wide(left[at][s : s + 1]), wide(right[at][s : s + 1])) for s in range(BLOCK)]
            for u in range(0, BLOCK, 2):
                v = u + 1
                inverse = reciprocal(p[u, u] * p[v, v] - p[u, v] * p[u, v])
                a00, a01, a11 = (p[v, v] * inverse, -p[u, v] * inverse, p[u, u] * inverse)
                within = p[u, v] * reciprocal(p[u, u])
                later = range(v + 1, BLOCK)
                t0 = {s: a00 * p[u, s] + a01 * p[v, s] for s in later}
                t1 = {s: a01 * p[u, s] + a11 * p[v, s] for s in later}
                for s in later:
                    for r in range(v + 1, s + 1):
                        p[r, s] = p[r, s] - (p[u, r] * t0[s] + p[v, r] * t1[s])
                    for i in below:
                        col[s][i] = col[s][i] - (col[u][i] * t0[s] + col[v][i] * t1[s])
                    lines[s] = tuple(
                        line - (t0[s] * first + t1[s] * second)
                        for line, first, second in zip(lines[s], lines[u], lines[v])
                    )
                for i in below:
                    f0 = col[u][i] * a00 + col[v][i] * a01
                    f1 = col[u][i] * a01 + col[v][i] * a11
                    left[i] = left[i] - (f0 * lines[u][0] + f1 * lines[v][0])
                    right[i] = right[i] - (f0 * lines[u][1] + f1 * lines[v][1])
                lines[v] = tuple(second - within * first for first, second in zip(lines[u], lines[v]))
            new_left, new_right = lines[0]
            for s in range(1, BLOCK):
                new_left = jnp.where(rows == s, lines[s][0], new_left)
                new_right = jnp.where(rows == s, lines[s][1], new_right)
            pivots = jnp.sum(jnp.where(lanes == column + rows, new_left, 0.0), axis=1, keepdims=True)
            scale = lax.rsqrt(pivots)
            left[at] = new_left * scale
            right[at] = new_right * scale
        left = jnp.concatenate(left, axis=0)
        right = jnp.concatenate(right, axis=0)
        finished.append(right)
        if base + PANEL < size:
            update = lax.dot_general(
                left[:, base + PANEL :],
                jnp.concatenate([left, right], axis=1),
                down,
                precision=HIGHEST,
                preferred_element_type=jnp.float32,
            )
            state = state[PANEL:] - update
    return jnp.concatenate(finished, axis=0)


def packed(matrix):
    half = matrix.shape[0] // 2
    rows = lax.broadcasted_iota(jnp.int32, (half, 2 * half), 0)
    lanes = lax.broadcasted_iota(jnp.int32, (half, 2 * half), 1)
    lower = pltpu.roll(matrix[half:], half, 1)
    diagonal = jnp.sum(jnp.where(lanes == rows, lower, 0.0), axis=0, keepdims=True)
    return jnp.concatenate(
        [jnp.where(lanes < rows, lower, matrix[:half]), jnp.broadcast_to(diagonal, (BLOCK, 2 * half))], axis=0
    )


def unpacked(values):
    size = values.shape[1]
    half = size // 2
    rows = lax.broadcasted_iota(jnp.int32, (half, size), 0)
    lanes = lax.broadcasted_iota(jnp.int32, (half, size), 1)
    entries = values[:half]
    diagonal = jnp.broadcast_to(values[half : half + 1], (half, size))
    lower = jnp.where(lanes < rows, entries, jnp.where(lanes == rows, diagonal, 0.0))
    part = jnp.concatenate([jnp.where(lanes >= rows, entries, 0.0), pltpu.roll(lower, half, 1)], axis=0)
    on = lax.broadcasted_iota(jnp.int32, (size, size), 0) == lax.broadcasted_iota(jnp.int32, (size, size), 1)
    return part + part.T - jnp.where(on, part, 0.0)


def rotate_kernel(frames, chunk, summed_ref, more_ref, sigma_ref, start_ref, coeffs_ref, basis_ref, basis_out, coeffs_out, sigma_out,
                  held_ref, turned_ref, come_sem, go_sem):
    come = pltpu.make_async_copy(basis_ref, held_ref, come_sem)
    come.start()
    size = summed_ref.shape[1]
    across = (((1,), (1,)), ((), ()))
    diagonal = lax.broadcasted_iota(jnp.int32, (size, size), 0) == lax.broadcasted_iota(jnp.int32, (size, size), 1)
    sigma = jnp.broadcast_to(sigma_ref[...], (size, size))
    gram = jnp.where(diagonal, sigma * sigma, 0.0) + unpacked(summed_ref[...] + more_ref[...]) * (1.0 / frames)

    def step(_, turned):
        return orthonormal_rows(jnp.dot(turned, gram, precision=HIGHEST, preferred_element_type=jnp.float32))

    turned = lax.fori_loop(0, ITERS, step, start_ref[...].T)
    rotation = turned.T
    high = rotation.astype(jnp.bfloat16)
    low = (rotation - high.astype(jnp.float32)).astype(jnp.bfloat16)
    pair = jnp.concatenate([high, low], axis=1)
    come.wait()
    goes = []
    for i in range(held_ref.shape[0] // chunk):
        at = pl.ds(i * chunk, chunk)
        total = jnp.dot(held_ref[at, :], pair, preferred_element_type=jnp.float32)
        turned_ref[at, :] = (total[:, :size] + total[:, size:]).astype(turned_ref.dtype)
        goes.append(pltpu.make_async_copy(turned_ref.at[at, :], basis_out.at[at, :], go_sem.at[i]))
        goes[-1].start()
    coeffs_out[...] = lax.dot_general(
        coeffs_ref[...], turned, across, precision=HIGHEST, preferred_element_type=jnp.float32
    )
    curved = jnp.dot(turned, gram, precision=HIGHEST, preferred_element_type=jnp.float32)
    sigma_out[...] = jnp.sqrt(jnp.sum((turned * curved).T, axis=0, keepdims=True))
    for go in goes:
        go.wait()


def rotated(summed_gram, more_gram, total_frames, prior_sigma, start_rotation, coeffs, basis):
    rows, size = basis.shape
    chunk = 1024 if rows % 1024 == 0 else rows
    inside = pl.BlockSpec(memory_space=pltpu.VMEM)
    outside = pl.BlockSpec(memory_space=pl.ANY)
    new_basis, new_coeffs, new_sigma = pl.pallas_call(
        functools.partial(rotate_kernel, total_frames, chunk),
        in_specs=[inside, inside, inside, inside, inside, outside],
        out_specs=(outside, inside, inside),
        out_shape=(
            jax.ShapeDtypeStruct(basis.shape, basis.dtype),
            jax.ShapeDtypeStruct(coeffs.shape, coeffs.dtype),
            jax.ShapeDtypeStruct((1, size), jnp.float32),
        ),
        scratch_shapes=[
            pltpu.VMEM(basis.shape, basis.dtype),
            pltpu.VMEM(basis.shape, basis.dtype),
            pltpu.SemaphoreType.DMA,
            pltpu.SemaphoreType.DMA((rows // chunk,)),
        ],
        compiler_params=pltpu.CompilerParams(vmem_limit_bytes=VMEM_BYTES),
        name="orthogonal_iteration",
    )(summed_gram, more_gram, prior_sigma.reshape(1, size), start_rotation, coeffs, basis)
    return (new_basis, new_coeffs, new_sigma.reshape(size))


def packed_alone(matrix):
    def kernel(matrix_ref, out_ref):
        out_ref[...] = packed(matrix_ref[...])

    size = matrix.shape[0]
    shape = jax.ShapeDtypeStruct((size // 2 + BLOCK, size), jnp.float32)
    return pl.pallas_call(kernel, out_shape=shape, name="pack")(matrix)


def gathered_body(raw_frames, dark_frame, dead_mask, frame_group, prior_sigma, start_rotation, basis):
    frame_count, strip_rows, columns = raw_frames.shape
    corrected = (
        (raw_frames.astype(jnp.float32) - dark_frame) * (1 - dead_mask).astype(jnp.float32)
    ).astype(jnp.bfloat16)
    position = jnp.arange(columns)
    offsets = position[None, :] - position[:, None]
    banded = jnp.zeros((columns, columns), jnp.float32)
    for shift_by in range(-3, 4):
        banded = banded + jnp.where(offsets == shift_by, BLUR_TAPS[shift_by + 3], 0.0)
    banded = banded.astype(jnp.bfloat16)
    column_blur = jnp.dot(
        corrected.reshape(frame_count * strip_rows, columns),
        banded,
        preferred_element_type=jnp.float32,
    )
    column_blur = column_blur.reshape(frame_count, strip_rows, columns)
    padded = extended(column_blur, (("strips", 1),), 3)
    row_blur = BLUR_TAPS[0] * padded[:, 0:strip_rows, :]
    for offset in range(1, 7):
        row_blur = row_blur + BLUR_TAPS[offset] * padded[:, offset : offset + strip_rows, :]
    frame_weight = jnp.power(
        jnp.float32(DECAY_RATE), (GROUPS - 1 - frame_group).astype(jnp.float32)
    )
    weighted = (
        (frame_weight[:, None, None] * row_blur)
        .astype(jnp.bfloat16)
        .reshape(frame_count, strip_rows * columns)
    )
    partial_value = jnp.dot(
        weighted,
        lax.all_gather(basis, "frames", axis=0, tiled=True),
        preferred_element_type=jnp.float32,
    )
    coeffs = lax.psum(partial_value, "strips")
    total_frames = frame_count * lax.axis_size("frames")
    local_gram = jnp.dot(coeffs.T, coeffs, precision=lax.Precision.HIGHEST)
    summed_gram = summed_over(local_gram, "frames")
    summed_gram = packed_alone(summed_gram)
    return rotated(summed_gram, jnp.zeros_like(summed_gram), total_frames, prior_sigma, start_rotation, coeffs, basis)


RING = (0, 2, 4, 6, 7, 5, 3, 1)
PLACES = 4 * len(RING) + 2
BAND = 16
EDGE = 8
FRAME_BLOCK = 16


def entry(place, at):
    index, table = place
    return table[index[0] * PLACES + at]


def blur_kernel(slot, outputs, begin, index_ref, table_ref, group_ref, main_ref, prev_ref, next_ref, *refs):
    place = (index_ref, table_ref)
    edge_ref, refs = (refs[0], refs[1:]) if slot else (None, refs)
    darks, masks, banded_ref, refs = (refs[:3], refs[3:6], refs[6], refs[7:])
    out_refs, (rows_ref, lines_ref, blurred_ref) = (refs[: len(outputs)], refs[len(outputs) :])
    side = entry(place, 4 * slot + 2)
    frames, height, columns = main_ref.shape
    span = height + 2 * EDGE
    parts = [main_ref[...], prev_ref[...], next_ref[...]]
    main, top, bottom = [
        (part.astype(jnp.float32) - dark_ref[...]) * (1 - mask_ref[...]).astype(jnp.float32)
        for part, dark_ref, mask_ref in zip(parts, darks, masks)
    ]
    top, bottom = (top[:, BAND - EDGE :], bottom[:, :EDGE])
    if slot:
        upper = entry(place, 0) == 0
        edge = edge_ref[...].astype(jnp.float32)
        top = jnp.where(entry(place, 4 * slot + 3) == 1, jnp.where(upper, 0.0, edge[:, BAND - EDGE :]), top)
        bottom = jnp.where(entry(place, 4 * slot + 4) == 1, jnp.where(upper, edge[:, :EDGE], 0.0), bottom)
    tiles = columns // 128
    flat_ref = rows_ref.reshape(tiles * frames * span, 128)
    for tile in range(tiles):
        part = slice(tile * 128, (tile + 1) * 128)
        rows_ref[tile, :, :EDGE] = top[:, :, part]
        rows_ref[tile, :, EDGE : EDGE + height] = main[:, :, part]
        rows_ref[tile, :, EDGE + height :] = bottom[:, :, part]
        for row in range(height + 6):
            line = flat_ref[pl.ds(tile * frames * span + row + EDGE - 3, frames, stride=span), :]
            lines_ref[row * frames : (row + 1) * frames, part] = line.astype(jnp.bfloat16)
    blurred_ref[...] = jnp.dot(lines_ref[...], banded_ref[...], preferred_element_type=jnp.float32)
    frame = lax.broadcasted_iota(jnp.int32, (frames, columns), 0)
    group = jnp.zeros((frames, columns), jnp.int32)
    for i in range(frames):
        group = jnp.where(frame == i, group_ref[pl.program_id(0) * frames + (begin + i)], group)
    weight = jnp.ones((frames, columns), jnp.float32)
    for value in range(GROUPS - 1):
        weight = jnp.where(group == value, DECAY_RATE ** (GROUPS - 1 - value), weight)
    for name, out_ref in zip(outputs, out_refs):
        first = 0 if len(outputs) == 1 else (side if name == "own" else 1 - side) * BAND
        for row in range(BAND):
            taken = [
                blurred_ref[pl.ds(pl.multiple_of((first + row + offset) * frames, frames), frames), :]
                for offset in range(7)
            ]
            total = BLUR_TAPS[3] * taken[3]
            for offset in range(3):
                total = total + BLUR_TAPS[offset] * (taken[offset] + taken[6 - offset])
            out_ref[row] = (weight * total).astype(jnp.bfloat16)


def blurred_bands(slot, outputs, begin, frame_count, place, raw_frames, edge, dark_frame, dead_mask, banded, frame_group):
    _, strip_rows, columns = raw_frames.shape
    bands = strip_rows // BAND
    height = len(outputs) * BAND
    skipped = begin // FRAME_BLOCK
    lines = height + 6

    def at_main(place):
        if len(outputs) == 2:
            return entry(place, 4 * slot + 1)
        side = entry(place, 4 * slot + 2)
        return 2 * entry(place, 4 * slot + 1) + (side if outputs[0] == "own" else 1 - side)

    at_prev = lambda place: jnp.maximum(len(outputs) * at_main(place) - 1, 0)
    at_next = lambda place: jnp.minimum(len(outputs) * (at_main(place) + 1), bands - 1)
    rows = ((height, at_main), (BAND, at_prev), (BAND, at_next))
    edges = () if edge is None else (edge,)

    def pixels(size, at):
        return pl.BlockSpec((size, columns), lambda f, index, table, group: (at((index, table)), 0))

    def frames(size, at):
        return pl.BlockSpec((FRAME_BLOCK, size, columns), lambda f, index, table, group: (f + skipped, at((index, table)), 0))

    grid_spec = pltpu.PrefetchScalarGridSpec(
        num_scalar_prefetch=3,
        grid=(frame_count // FRAME_BLOCK,),
        in_specs=[frames(*row) for row in rows]
        + [frames(BAND, lambda place: 0)] * len(edges)
        + [pixels(*row) for row in rows] * 2
        + [pl.BlockSpec(banded.shape, lambda f, index, table, group: (0, 0))],
        out_specs=[pl.BlockSpec((BAND, FRAME_BLOCK, columns), lambda f, index, table, group: (0, f, 0))] * len(outputs),
        scratch_shapes=[
            pltpu.VMEM((columns // 128, FRAME_BLOCK, height + 2 * EDGE, 128), jnp.float32),
            pltpu.VMEM((lines * FRAME_BLOCK, columns), jnp.bfloat16),
            pltpu.VMEM((lines * FRAME_BLOCK, columns), jnp.float32),
        ],
    )
    shape = jax.ShapeDtypeStruct((BAND, frame_count, columns), jnp.bfloat16)
    starts = slot == 0 and outputs[0] == "sent"
    return pl.pallas_call(
        functools.partial(blur_kernel, slot, outputs, begin),
        grid_spec=grid_spec,
        out_shape=[shape] * len(outputs),
        compiler_params=pltpu.CompilerParams(vmem_limit_bytes=60 * 1024 * 1024 if starts else BLUR_BYTES),
        cost_estimate=pl.CostEstimate(flops=1024, bytes_accessed=1024, transcendentals=0),
        name="blur_bands",
    )(*place, frame_group, *[raw_frames] * 3, *edges, *[dark_frame] * 3, *[dead_mask] * 3, banded)


def project_kernel(slot, at, parts, index_ref, table_ref, total_ref, *refs):
    line_refs, basis_refs, out_ref = (refs[:parts], refs[parts:-1], refs[-1])
    columns = line_refs[0].shape[2]

    @pl.when(pl.program_id(0) == 0)
    def _():
        out_ref[...] = total_ref[...]

    def add(basis_ref):
        total = out_ref[at, :]
        for row in range(line_refs[0].shape[0]):
            lines = jnp.concatenate([line_ref[row] for line_ref in line_refs], axis=0)
            total = total + jnp.dot(
                lines, basis_ref[row * columns : (row + 1) * columns, :], preferred_element_type=jnp.float32
            )
        out_ref[at, :] = total

    if len(basis_refs) == 1:
        add(basis_refs[0])
    else:
        here = entry((index_ref, table_ref), PLACES - 1) == slot
        pl.when(here)(lambda: add(basis_refs[0]))
        pl.when(jnp.logical_not(here))(lambda: add(basis_refs[1]))


def projected(total, own, came, basis, first_row, choice=None):
    step = 4
    begin = 0 if own else total.shape[0] // 2
    lines = (*own, *came)
    columns = lines[0].shape[2]
    at = slice(begin, begin + sum(values.shape[1] for values in lines))
    size = basis.shape[1]
    skipped = first_row // step
    steps = basis.shape[0] // columns // step
    whole = pl.BlockSpec(total.shape, lambda i, index, table: (0, 0))
    other, place, slot = choice or (None, [jnp.zeros((1,), jnp.int32)] * 2, 0)
    blocks = (basis,) if choice is None else (basis, other)
    return pl.pallas_call(
        functools.partial(project_kernel, slot, at, len(lines)),
        grid_spec=pltpu.PrefetchScalarGridSpec(
            num_scalar_prefetch=2,
            grid=(steps,),
            in_specs=[whole]
            + [pl.BlockSpec((step, *values.shape[1:]), lambda i, index, table: (i + skipped, 0, 0)) for values in lines]
            + [pl.BlockSpec((step * columns, size), lambda i, index, table: (i, 0))] * len(blocks),
            out_specs=whole,
        ),
        out_shape=jax.ShapeDtypeStruct(total.shape, jnp.float32),
        compiler_params=pltpu.CompilerParams(vmem_limit_bytes=VMEM_BYTES),
        cost_estimate=pl.CostEstimate(flops=1024, bytes_accessed=1024, transcendentals=0),
        name="project_band",
    )(*place, total, *lines, *blocks)


def merge_kernel(total_ref, strip_ref, side_ref, both_ref, coeffs_out, gram_out):
    half = coeffs_out.shape[0]
    down = (((0,), (0,)), ((), ()))
    near = total_ref[...] + strip_ref[...]
    far = side_ref[...] + both_ref[...]
    grams = []
    for at, other in ((slice(0, half), slice(half, None)), (slice(half, None), slice(0, half))):
        coeffs = near[at] + far[other]
        if not grams:
            coeffs_out[...] = coeffs
        grams.append(lax.dot_general(coeffs, coeffs, down, precision=HIGHEST, preferred_element_type=jnp.float32))
    gram_out[...] = packed(grams[0] + grams[1])


def placement():
    ring = len(RING)
    table = np.zeros((2 * ring, 2, PLACES), np.int32)
    for at in range(ring):
        order = [0, -1, 1, -2, 2, -3, 3, 4]
        if RING[at] in (0, ring - 1):
            order[:2] = order[1::-1]
        for strip in range(2):
            for x in range(2):
                row = table[2 * RING[at] + x, strip]
                row[0], row[-1] = (strip, order.index(0))
                for slot, by in enumerate(order):
                    pair = RING[(at + by) % ring]
                    row[4 * slot + 1 : 4 * slot + 5] = (pair, x, pair == 0, pair == ring - 1)
    return table.reshape(-1)


def paired_body(raw_frames, dark_frame, dead_mask, frame_group, prior_sigma, start_rotation, basis):
    frame_count, strip_rows, columns = raw_frames.shape
    size = basis.shape[1]
    count = lax.axis_size("frames")
    strips = lax.axis_size("strips")
    ring = len(RING)
    strip = lax.axis_index("strips")
    index = lax.axis_index(("frames", "strips"))
    place = (index.reshape(1).astype(jnp.int32), jnp.asarray(placement()))

    def links(by):
        return [
            (2 * RING[at] + x, 2 * RING[(at + by) % ring] + x) for at in range(ring) for x in range(2)
        ]

    swap = [(i, i ^ 1) for i in range(count)]
    move = lambda values, pairs: lax.ppermute(values, "frames", pairs)
    column = np.arange(columns)
    taps = np.array(BLUR_TAPS + (0.0,), np.float32)
    offsets = column[None, :] - column[:, None] + 3
    banded = jnp.asarray(taps[np.where((offsets >= 0) & (offsets < 7), offsets, 7)], jnp.bfloat16)

    def bands(slot, outputs, edge, begin=0, held=frame_count):
        return blurred_bands(
            slot, outputs, begin, held, place, raw_frames, edge, dark_frame, dead_mask, banded, frame_group
        )

    first = frame_count // 2
    (sent_first,) = bands(0, ("sent",), None, 0, first)
    sent_first, near_raw, near_dark, near_mask = lax.optimization_barrier(
        (sent_first, raw_frames, dark_frame, dead_mask)
    )
    came_first = move(sent_first, swap)
    (sent_rest,) = bands(0, ("sent",), None, first, first)
    near = jnp.where(strip == 0, strip_rows - BAND, 0)
    rows = [lax.dynamic_slice_in_dim(values, near, BAND, axis=-2) for values in (near_raw, near_dark, near_mask)]
    border = ((rows[0].astype(jnp.float32) - rows[1]) * (1 - rows[2]).astype(jnp.float32)).astype(jnp.bfloat16)
    came_first, sent_rest, border, passing = lax.optimization_barrier((came_first, sent_rest, border, basis))
    came_rest = move(sent_rest, swap)
    edge = lax.ppermute(border, "strips", [(0, 1), (1, 0)])
    sent_next, own_next = bands(1, ("sent", "own"), edge)
    came_rest, sent_next, own_next = lax.optimization_barrier((came_rest, sent_next, own_next))
    half = basis.shape[0] // 2
    blocks = {0: basis}
    send, own, came = ([None, sent_next], [None, own_next], [came_rest])
    total = jnp.zeros((2 * frame_count, size), jnp.float32)
    up, down = (passing, passing)

    def project(total, slot):
        parts = (came[slot],) if slot else (came_first, came[0])
        if slot < 2:
            return projected(total, (own[slot],), parts, blocks[0], 0, (blocks[-1], place, slot))
        return projected(total, (own[slot],), parts, blocks[(0, -1, 1, -2, 2, -3, 3)[slot]], 0)

    for stage in range(4):
        if stage < 3:
            up, down = (move(up, links(1)), move(down, links(-1)))
        else:
            up, down = (move(up[:half], links(1)), move(down[half:], links(-1)))
        for slot in range(len(came), min(2 * stage + 3, ring)):
            if slot == len(send):
                sent, kept = bands(slot, ("sent", "own"), edge)
                own.append(kept)
                send.append(sent)
            came.append(move(send[slot], swap))
        if stage == 0:
            (own[0],) = bands(0, ("own",), None)
        while stage < 2 and len(own) < (5, 8)[stage]:
            sent, kept = bands(len(own), ("sent", "own"), edge)
            own.append(kept)
            send.append(sent)
        for slot in ((), (0, 1, 2), (3, 4), (5, 6))[stage]:
            total = project(total, slot)
        if stage == 3:
            break
        last = len(came)
        held = (up, down, total, came[last - 2], came[last - 1]) + tuple(send[last:]) + tuple(own[last:])
        up, down, total, came[last - 2], came[last - 1], *others = lax.optimization_barrier(held)
        waiting = len(send) - last
        send[last:] = others[:waiting]
        own[last:] = others[waiting:]
        blocks[-stage - 1], blocks[stage + 1] = (up, down)
    for lines in (((own[7],), ()), ((), (came[7],))):
        for n, block in enumerate((up, down)):
            total = projected(total, *lines, block, n * BAND // 2)
    flips = [
        lax.ppermute(total, ("frames", "strips"), [(i, i ^ flip) for i in range(count * strips)]) for flip in (1, 2, 3)
    ]
    coeffs, gram = pl.pallas_call(
        merge_kernel,
        out_shape=(
            jax.ShapeDtypeStruct((frame_count, size), jnp.float32),
            jax.ShapeDtypeStruct((size // 2 + BLOCK, size), jnp.float32),
        ),
        name="merge",
    )(total, *flips)
    near = [move(gram, [(i, i ^ flip) for i in range(count)]) for flip in (2, 4, 6)]
    gram = (gram + near[0]) + (near[1] + near[2])
    far = move(gram, [(i, i ^ 8) for i in range(count)])
    return rotated(gram, far, frame_count * count, prior_sigma, start_rotation, coeffs, basis)


def body(raw_frames, *others):
    _, strip_rows, columns = raw_frames.shape
    paired = lax.axis_size("frames") == 2 * len(RING) and lax.axis_size("strips") == 2
    if paired and strip_rows == 2 * len(RING) * BAND and raw_frames.shape[0] % FRAME_BLOCK == 0:
        return paired_body(raw_frames, *others)
    return gathered_body(raw_frames, *others)


def solution(mesh):
    placed = (
        P("frames", "strips", None),
        P("strips", None),
        P("strips", None),
        P("frames"),
        P(),
        P(),
        P(("strips", "frames"), None),
    )
    return jax.shard_map(
        body,
        mesh=mesh,
        in_specs=placed,
        out_specs=(P(("strips", "frames"), None), P("frames", None), P()),
        check_vma=False,
    )
```
